512 devices in a mesh: slab: 512 (over y, z, x, core).
Axes of the slice: x: 4, y: 4, z: 16, core: 2. Of those that a mesh axis runs over, the one named last changes fastest.
Arguments:
- start_vectors: float32 [32, 1024, 4096], P(None, 'slab'), may hold values from -120 to 120, as said below
- materials: int32 [1024, 4096], P('slab'), may hold values from 0 to 7
- conduct_table: float32 [8], replicated, may hold values from 0.1 to 10
- aggregate_ids: int32 [8192], P('slab'), may hold values from 0 to 4095, never falling along the last dimension, each value on 1 to 16 neighbouring positions
Outputs:
- prolongator: float32 [32, 1024, 4096], P(None, 'slab')
- coarse_factors: float32 [8192, 32, 32], P('slab')
The draws below stay inside these ranges and needn't reach their ends.
Inputs may be any that keep to these rules, and one draw needn't show every extreme that they name: `start_vectors`: built from normal or uniform values; rows differ in scale. `aggregate_ids`: aggregate numbers never fall along the blocks; each aggregate is 1 to 16 consecutive blocks, and one is exactly 16.
All inputs are finite; a program needn't handle non-finite values.
Results may differ from the reference program's by a relative error of at most 0.0003.
Values sent between devices are 32-bit elements; how exact they have to be, the bound alone decides.
A program may use at most 64 MiB of HBM per device.

```python
import math
import jax
import jax.numpy as jnp
import numpy as np
from jax import lax

K = 32
BLKR = 512
NX = 256
SWEEPS = 4
NMAT = 8
PLANE = 4096
NZ = 1024
BLK_DEV = 16
NB = 8192
AGGS = 4096


def draw_start_vectors(key, part):
    noise_key, scale_key = jax.random.split(key, 2)
    depth = jnp.arange(NZ).astype(jnp.float32) / (NZ - 1)
    colscale = jnp.exp(jax.random.uniform(scale_key, (K, 1, 1), jnp.float32, 0.0, 2.302585))
    amplitude = 1.0 + 2.0 * depth
    noise = jnp.clip(jax.random.normal(noise_key, (K, NZ, PLANE), jnp.float32), -4.0, 4.0)
    return (noise * amplitude[None, :, None] * colscale).astype(jnp.float32)


def place_ends(result, rng, low, high):
    longest = result.shape.index(max(result.shape))
    spots = []
    for shift in (0, 1):
        where = [jax.random.randint(jax.random.fold_in(rng, axis), (), 0, length) for axis, length in enumerate(result.shape)]
        where[longest] = (where[longest] + shift) % result.shape[longest]
        spots.append(tuple(where))
    return result.at[spots[0]].set(low).at[spots[1]].set(high)


def length_profile(number_of, total, limit, slope):
    weights = [(1 << 20) // math.isqrt(rank ** slope) + 1 for rank in range(2, number_of + 1)]
    rest, given = total - limit - (number_of - 1), [1] * (number_of - 1)
    while rest > 0:
        movable = [i for i in range(number_of - 1) if given[i] < limit]
        pool, left = sum([weights[i] for i in movable]), rest
        for i in movable:
            extra = min(limit - given[i], max(1, left * weights[i] // pool), rest)
            given[i] = given[i] + extra
            rest = rest - extra
    return np.array([limit] + given)


def ragged_sizes(own_key, amount, total, reach, skew):
    if amount == 2:
        one = jax.random.randint(own_key, (), max(1, total - reach), min(reach, total - 1) + 1)
        return jnp.stack([one, total - one])
    lengths = jnp.asarray(length_profile(amount, total, reach, skew), jnp.int32)
    couples = (amount - 1) // 2
    donor, sink = lengths[1:1 + 2 * couples:2], lengths[2:2 + 2 * couples:2]
    margin = jnp.minimum(donor - 1, reach - sink)
    passed = jax.random.randint(jax.random.fold_in(own_key, 1), (couples,), 0, 1 << 20) % (margin + 1)
    lengths = lengths.at[1:1 + 2 * couples:2].set(donor - passed).at[2:2 + 2 * couples:2].set(sink + passed)
    return lengths[jax.random.permutation(jax.random.fold_in(own_key, 2), amount)]


def setup_inputs(seed: int = 0) -> dict:
    seeds = jax.random.split(jax.random.key(seed), 5)
    return {
        "start_vectors": draw_start_vectors(jax.random.fold_in(seeds[4], 71), 0),
        "materials": place_ends(jax.random.randint(seeds[1], (NZ, PLANE), 0, NMAT), jax.random.fold_in(seeds[1], 1), 0, NMAT - 1).astype(jnp.int32),
        "conduct_table": jnp.clip(jnp.exp(jax.random.uniform(seeds[2], (NMAT,), jnp.float32, math.log(0.1), math.log(10.0))), 0.1, 10.0),
        "aggregate_ids": jnp.searchsorted(jnp.cumsum(ragged_sizes(seeds[3], AGGS, NB, BLK_DEV, 2)), jnp.arange(NB), side="right").astype(jnp.int32),
    }


relax_weight = 2.0 / 3.0
epsilon = 1e-06

def shifted(values, offset, x_mask):
    padding = jnp.zeros(values.shape[:-1] + (abs(offset),), values.dtype)
    if offset > 0:
        moved_vals = jnp.concatenate([values[..., offset:], padding], axis=-1)
    else:
        moved_vals = jnp.concatenate([padding, values[..., :offset]], axis=-1)
    return moved_vals * x_mask

def plane_masks(plane_len):
    xpos = jnp.arange(plane_len) % NX
    west = (xpos > 0).astype(jnp.float32)
    east = (xpos < NX - 1).astype(jnp.float32)
    return (west, east, jnp.ones((plane_len,), jnp.float32))

def face_coef(cond, other):
    return jnp.where(other > 0.0, 2.0 * cond * other / (cond + other), cond)

def coefficients(cond_ext):
    west, east, unity = plane_masks(cond_ext.shape[-1])
    inner = cond_ext[1:-1]
    coef_down = face_coef(inner, cond_ext[:-2])
    coef_up = face_coef(inner, cond_ext[2:])
    coef_west = face_coef(inner, shifted(inner, -1, west))
    coef_east = face_coef(inner, shifted(inner, 1, east))
    coef_south = face_coef(inner, shifted(inner, -NX, unity))
    coef_north = face_coef(inner, shifted(inner, NX, unity))
    diag_sum = coef_down + coef_up + coef_west + coef_east + coef_south + coef_north
    exists = inner > 0.0
    diag_safe = jnp.where(exists, diag_sum, 1.0)
    return (coef_down, coef_up, coef_west, coef_east, coef_south, coef_north, diag_safe, exists)

def jacobi_step(extended, coefs):
    west, east, unity = plane_masks(extended.shape[-1])
    inner = extended[:, 1:-1]
    neigh = coefs[0] * extended[:, :-2] + coefs[1] * extended[:, 2:]
    neigh = neigh + coefs[2] * shifted(inner, -1, west) + coefs[3] * shifted(inner, 1, east)
    neigh = neigh + coefs[4] * shifted(inner, -NX, unity) + coefs[5] * shifted(inner, NX, unity)
    return inner - relax_weight * (coefs[6] * inner - neigh) / coefs[6]

def reference(start_vectors, materials, conduct_table, aggregate_ids):
    conduct = conduct_table[materials]
    coefs = coefficients(jnp.pad(conduct, ((1, 1), (0, 0))))
    vectors = start_vectors
    for sweep in range(SWEEPS):
        vectors = jacobi_step(jnp.pad(vectors, ((0, 0), (1, 1), (0, 0))), coefs)
    mean_sq = lax.optimization_barrier(jnp.sum(vectors * vectors, axis=(1, 2))) / (NZ * PLANE)
    root_mean = jnp.sqrt(mean_sq + epsilon)
    scaled = vectors / root_mean[:, None, None]
    blocks = jnp.transpose(scaled.reshape(K, NB, BLKR), (1, 0, 2))
    grams = jnp.einsum('bkr,blr->bkl', blocks, blocks, precision=lax.Precision.HIGHEST) / BLKR
    agg_grams = jax.ops.segment_sum(grams, aggregate_ids, num_segments=AGGS)
    lower_fac = jnp.linalg.cholesky(agg_grams[aggregate_ids])
    solved = lax.linalg.triangular_solve(lower_fac, blocks, left_side=True, lower=True)
    prolongator = jnp.transpose(solved, (1, 0, 2)).reshape(K, NZ, PLANE)
    return (prolongator, jnp.transpose(lower_fac, (0, 2, 1)))
```

```python
import functools

import jax
import jax.numpy as jnp
from jax import lax
from jax.experimental import pallas as pl
from jax.experimental.pallas import tpu as pltpu
from jax.sharding import PartitionSpec as P

K = 32
BLKR = 512
NX = 256
NY = 16
PLANE = NX * NY
SWEEPS = 4
NMAT = 8
GROUP = 8
GROUPS = K // GROUP
BLOCKS = 16
PLANES = 2
CELLS = 1024 * PLANE

WEIGHT = 2.0 / 3.0
EPS = 1e-06
LIFT = 2.0**20


def reduce_groups(n):
    return ((1, 8), (128, 4), (8, 16)) if n == 512 else ((1, n),)


def kernel(
    n, sv, mat, table, ids, out, coarse,
    vec, halo, coef, cond, cond_out, cond_in, id_out, id_in,
    edge_out, edge_in, aug, rows, halves, sums, sums_in,
    load_sem, send_sem, recv_sem, small_send, small_recv, ar_send, ar_recv,
):
    me = lax.axis_index("slab")
    right, left = lax.rem(me + 1, n), lax.rem(me + n - 1, n)
    sides = (left, right)
    steps = reduce_groups(n)

    def partner(step, d):
        stride, size = steps[step]
        pos = lax.rem(lax.div(me, stride), size)
        return me + (lax.rem(pos + d, size) - pos) * stride

    def remote(src, dst, ssem, rsem, dev):
        return pltpu.make_async_remote_copy(
            src_ref=src, dst_ref=dst, send_sem=ssem, recv_sem=rsem,
            device_id=(dev,), device_id_type=pl.DeviceIdType.MESH,
        )

    barrier = pltpu.get_barrier_semaphore()
    count = 0
    targets = [left, right]
    for step, (_, size) in enumerate(steps):
        targets += [partner(step, d) for d in range(1, size)]
    for dev in targets:
        pl.semaphore_signal(barrier, inc=1, device_id=(dev,), device_id_type=pl.DeviceIdType.MESH)
        count += 1

    load = pltpu.make_async_copy(sv, vec.at[0], load_sem)
    load.start()

    for z in range(PLANES):
        for y in range(NY):
            cols = slice(y * NX, (y + 1) * NX)
            m = jnp.broadcast_to(mat[z : z + 1, cols], (8, NX))
            k = jnp.zeros((8, NX), jnp.float32)
            for j in range(NMAT):
                k = jnp.where(m == j, table[j], k)
            cond[z, :, cols] = k
            cond_out[z, :, cols] = k[0:1]
    id_out[0] = jnp.full((8, 128), ids[0], jnp.int32)
    id_out[1] = jnp.full((8, 128), ids[BLOCKS - 1], jnp.int32)

    pl.semaphore_wait(barrier, count)
    load.wait()

    small = []
    for z in range(PLANES):
        small.append(remote(cond_out.at[z], cond_in.at[1 - z], small_send.at[z], small_recv.at[z], sides[z]))
        small.append(remote(id_out.at[z], id_in.at[1 - z], small_send.at[2 + z], small_recv.at[2 + z], sides[z]))
    for c in small:
        c.start()

    def plane_copy(s, q, z):
        lanes = pl.ds(pl.multiple_of(q * GROUP, GROUP), GROUP)
        return remote(
            vec.at[s, z, lanes], halo.at[s, 1 - z, lanes],
            send_sem.at[s, q, z], recv_sem.at[s, q, z], sides[z],
        )

    for q in range(GROUPS):
        for z in range(PLANES):
            plane_copy(0, q, z).start()

    for c in small:
        c.wait_recv()

    has_below = (me > 0).astype(jnp.float32)
    has_above = (me < n - 1).astype(jnp.float32)
    xpos = lax.broadcasted_iota(jnp.int32, (8, NX), 1)
    west_ok, east_ok = xpos > 0, xpos < NX - 1

    def face(k, other):
        return 2.0 * k * other / (k + other)

    for z in range(PLANES):
        for y in range(NY):
            cols = slice(y * NX, (y + 1) * NX)
            k = cond[z, :, cols]
            zero = jnp.zeros_like(k)
            fw = face(k, pltpu.roll(k, 1, axis=1))
            fe = face(k, pltpu.roll(k, NX - 1, axis=1))
            fs = face(k, cond[z, :, (y - 1) * NX : y * NX]) if y > 0 else k
            fn = face(k, cond[z, :, (y + 1) * NX : (y + 2) * NX]) if y < NY - 1 else k
            below = cond[0, :, cols] if z == 1 else jnp.broadcast_to(cond_in[0, :, cols], (8, NX))
            above = cond[1, :, cols] if z == 0 else jnp.broadcast_to(cond_in[1, :, cols], (8, NX))
            fd, fu = face(k, below), face(k, above)
            hd = has_below if z == 0 else 1.0
            hu = has_above if z == 1 else 1.0
            dsum = (
                jnp.where(west_ok, fw, k) + jnp.where(east_ok, fe, k) + fs + fn
                + (hd * fd + (1.0 - hd) * k) + (hu * fu + (1.0 - hu) * k)
            )
            scale = WEIGHT / dsum
            coef[z, 0, :, cols] = jnp.where(west_ok, fw * scale, zero)
            coef[z, 1, :, cols] = jnp.where(east_ok, fe * scale, zero)
            coef[z, 2, :, cols] = fs * scale
            coef[z, 3, :, cols] = fn * scale
            coef[z, 4, :, cols] = fd * scale * hd
            coef[z, 5, :, cols] = fu * scale * hu

    def sweep(t, carry):
        s, q = lax.div(t, GROUPS), lax.rem(t, GROUPS)
        lanes = pl.ds(pl.multiple_of(q * GROUP, GROUP), GROUP)
        for z in range(PLANES):
            plane_copy(s, q, z).wait_recv()
        for z in range(PLANES):
            for y in range(NY):
                cols = slice(y * NX, (y + 1) * NX)
                c = vec[s, z, lanes, cols]
                acc = c * (1.0 - WEIGHT)
                acc += coef[z, 0, :, cols] * pltpu.roll(c, 1, axis=1)
                acc += coef[z, 1, :, cols] * pltpu.roll(c, NX - 1, axis=1)
                if y > 0:
                    acc += coef[z, 2, :, cols] * vec[s, z, lanes, (y - 1) * NX : y * NX]
                if y < NY - 1:
                    acc += coef[z, 3, :, cols] * vec[s, z, lanes, (y + 1) * NX : (y + 2) * NX]
                below = vec[s, 0, lanes, cols] if z == 1 else halo[s, 0, lanes, cols]
                above = vec[s, 1, lanes, cols] if z == 0 else halo[s, 1, lanes, cols]
                acc += coef[z, 4, :, cols] * below
                acc += coef[z, 5, :, cols] * above
                vec[s + 1, z, lanes, cols] = acc

            @pl.when(s < SWEEPS - 1)
            def _():
                plane_copy(s + 1, q, z).start()

        return carry

    lax.fori_loop(0, SWEEPS * GROUPS, sweep, 0)

    nt = (((1,), (1,)), ((), ()))
    dot = functools.partial(lax.dot_general, preferred_element_type=jnp.float32)
    local = []
    for b in range(BLOCKS):
        z, c = divmod(b, PLANE // BLKR)
        v = vec[SWEEPS, z, :, c * BLKR : (c + 1) * BLKR] * LIFT
        hi = v.astype(jnp.bfloat16)
        lo = (v - hi.astype(jnp.float32)).astype(jnp.bfloat16)
        halves[b, 0:K] = hi
        halves[b, K : 2 * K] = lo
        g = dot(hi, hi, nt) + dot(hi, lo, nt) + dot(lo, hi, nt)
        local.append(g * (1.0 / BLKR))

    same = [None] + [(ids[b] == ids[b - 1]).astype(jnp.float32) for b in range(1, BLOCKS)]
    run = [local[0]]
    for b in range(1, BLOCKS):
        run.append(local[b] + same[b] * run[b - 1])
    for b in range(BLOCKS - 2, -1, -1):
        run[b] = run[b] + same[b + 1] * (run[b + 1] - run[b])
    edge_out[0] = run[0]
    edge_out[1] = run[BLOCKS - 1]
    edges = [remote(edge_out.at[z], edge_in.at[1 - z], small_send.at[4 + z], small_recv.at[4 + z], sides[z]) for z in range(PLANES)]
    for c in edges:
        c.start()

    total = local[0]
    for b in range(1, BLOCKS):
        total = total + local[b]
    i_pos = lax.broadcasted_iota(jnp.int32, (K, K), 0)
    j_pos = lax.broadcasted_iota(jnp.int32, (K, K), 1)
    diag = jnp.sum(jnp.where(i_pos == j_pos, total, 0.0), axis=0, keepdims=True)
    diag = jnp.concatenate([diag, jnp.zeros((1, 128 - K), jnp.float32)], axis=1)
    sums[0] = jnp.broadcast_to(diag, (8, 128))

    slot0 = [sum(size - 1 for _, size in steps[:step]) for step in range(len(steps))]

    def reduce_copy(step, d):
        slot = slot0[step] + d - 1
        return remote(sums.at[step], sums_in.at[slot], ar_send.at[slot], ar_recv.at[slot], partner(step, d))

    def reduce_send(step):
        for d in range(1, steps[step][1]):
            reduce_copy(step, d).start()

    def reduce_recv(step):
        tot = sums[step]
        for d in range(1, steps[step][1]):
            reduce_copy(step, d).wait_recv()
            tot = tot + sums_in[slot0[step] + d - 1]
        sums[step + 1] = tot

    reduce_send(0)

    for c in edges:
        c.wait_recv()
    pad = jnp.zeros((K, 2 * K), jnp.float32)
    end = jnp.zeros((K, K), jnp.float32)
    for b in range(BLOCKS):
        from_left = jnp.where(id_in[0, 0:1, 0:K] == ids[b], 1.0, 0.0) * has_below
        from_right = jnp.where(id_in[1, 0:1, 0:K] == ids[b], 1.0, 0.0) * has_above
        g = run[b] + from_left * edge_in[0] + from_right * edge_in[1]
        aug[pl.ds(b, K, stride=BLOCKS), :] = jnp.concatenate([pad, g, end], axis=1)

    lane = lax.broadcasted_iota(jnp.int32, (BLOCKS, 128), 1)
    r = [
        aug[i * BLOCKS : (i + 1) * BLOCKS, :] + jnp.where((lane == i) | (lane == K + i), 1.0, 0.0)
        for i in range(K)
    ]
    done = 0
    for k in range(K):
        d = jnp.broadcast_to(r[k][:, 2 * K + k : 2 * K + k + 1], (BLOCKS, 128))
        scaled = r[k] / d
        for i in range(k + 1, K):
            r[i] = r[i] - jnp.broadcast_to(r[k][:, 2 * K + i : 2 * K + i + 1], (BLOCKS, 128)) * scaled
        keep = (lane < 2 * K) | (lane >= 2 * K + k)
        rows[k * BLOCKS : (k + 1) * BLOCKS, :] = jnp.where(keep, r[k] * lax.rsqrt(d), 0.0)
        if k % 8 == 7 and done < len(steps) - 1:
            reduce_recv(done)
            done += 1
            reduce_send(done)

    for b in range(BLOCKS):
        z, c = divmod(b, PLANE // BLKR)
        w = rows[pl.ds(b, K, stride=BLOCKS), :][:, 0 : 2 * K]
        hi = w.astype(jnp.bfloat16)
        lo = (w - hi.astype(jnp.float32)).astype(jnp.bfloat16)
        nn = (((1,), (0,)), ((), ()))
        x = halves[b]
        out[z, :, c * BLKR : (c + 1) * BLKR] = dot(hi, x, nn) + dot(lo, x, nn)

    while done < len(steps):
        reduce_recv(done)
        done += 1
        if done < len(steps):
            reduce_send(done)
    mean_sq = sums[len(steps)][0:1, 0:K] * (BLKR / CELLS)
    inv = lax.rsqrt(mean_sq + EPS * LIFT * LIFT)
    for b in range(BLOCKS):
        coarse[b] = rows[pl.ds(b, K, stride=BLOCKS), :][:, 2 * K : 3 * K] * inv

    for c in small + edges:
        c.wait_send()
    for step, (_, size) in enumerate(steps):
        for d in range(1, size):
            reduce_copy(step, d).wait_send()

    def drain(t, carry):
        for z in range(PLANES):
            plane_copy(lax.div(t, GROUPS), lax.rem(t, GROUPS), z).wait_send()
        return carry

    lax.fori_loop(0, SWEEPS * GROUPS, drain, 0)


def local(n, start_vectors, materials, conduct_table, aggregate_ids):
    f32 = jnp.float32
    steps = reduce_groups(n)
    slots = sum(size - 1 for _, size in steps)
    vmem, smem = pl.BlockSpec(memory_space=pltpu.VMEM), pl.BlockSpec(memory_space=pltpu.SMEM)
    out, coarse = pl.pallas_call(
        functools.partial(kernel, n),
        out_shape=(
            jax.ShapeDtypeStruct((PLANES, K, PLANE), f32),
            jax.ShapeDtypeStruct((BLOCKS, K, K), f32),
        ),
        in_specs=[pl.BlockSpec(memory_space=pl.ANY), vmem, smem, smem],
        out_specs=(vmem, vmem),
        scratch_shapes=[
            pltpu.VMEM((SWEEPS + 1, PLANES, K, PLANE), f32),
            pltpu.VMEM((SWEEPS, 2, K, PLANE), f32),
            pltpu.VMEM((PLANES, 6, 8, PLANE), f32),
            pltpu.VMEM((PLANES, 8, PLANE), f32),
            pltpu.VMEM((PLANES, 1, PLANE), f32),
            pltpu.VMEM((2, 1, PLANE), f32),
            pltpu.VMEM((2, 8, 128), jnp.int32),
            pltpu.VMEM((2, 8, 128), jnp.int32),
            pltpu.VMEM((2, K, K), f32),
            pltpu.VMEM((2, K, K), f32),
            pltpu.VMEM((K * BLOCKS, 128), f32),
            pltpu.VMEM((K * BLOCKS, 128), f32),
            pltpu.VMEM((BLOCKS, 2 * K, BLKR), jnp.bfloat16),
            pltpu.VMEM((len(steps) + 1, 8, 128), f32),
            pltpu.VMEM((slots, 8, 128), f32),
            pltpu.SemaphoreType.DMA,
            pltpu.SemaphoreType.DMA((SWEEPS, GROUPS, PLANES)),
            pltpu.SemaphoreType.DMA((SWEEPS, GROUPS, PLANES)),
            pltpu.SemaphoreType.DMA((6,)),
            pltpu.SemaphoreType.DMA((6,)),
            pltpu.SemaphoreType.DMA((slots,)),
            pltpu.SemaphoreType.DMA((slots,)),
        ],
        compiler_params=pltpu.CompilerParams(
            collective_id=0, has_side_effects=True, vmem_limit_bytes=40 * 2**20
        ),
        name="adaptive_setup",
    )(jnp.transpose(start_vectors, (1, 0, 2)), materials, conduct_table, aggregate_ids)
    return jnp.transpose(out, (1, 0, 2)), coarse


def solution(mesh):
    n = mesh.shape["slab"]
    return jax.shard_map(
        functools.partial(local, n),
        mesh=mesh,
        in_specs=(P(None, "slab", None), P("slab", None), P(), P("slab")),
        out_specs=(P(None, "slab", None), P("slab", None, None)),
        check_vma=False,
    )
```

```python
import functools

import jax
import jax.numpy as jnp
from jax import lax
from jax.experimental import pallas as pl
from jax.experimental.pallas import tpu as pltpu
from jax.sharding import PartitionSpec as P

K = 32
BLKR = 512
NX = 256
NY = 16
PLANE = NX * NY
SWEEPS = 4
NMAT = 8
GROUP = 8
GROUPS = K // GROUP
BLOCKS = 16
PLANES = 2
CELLS = 1024 * PLANE

WEIGHT = 2.0 / 3.0
EPS = 1e-06
LIFT = 2.0**20


CORE, X, Y, Z = (1, 2), (2, 4), (128, 4), (8, 16)
STEPS = ((CORE,), (X, Y), (Z,))
ENTRY = ((X, 1), (X, 3), (Y, 1), (Y, 3), (Z, 1), (Z, 15))
TOKENS = (ENTRY, ((X, 1), (X, 2), (X, 3), (Z, 2), (Z, 14)), ((Z, 4), (Z, 12)))


def peers(step):
    found = [()]
    for axis in step:
        found = [f + ((axis, d),) for f in found for d in range(axis[1])]
    return [tuple(move for move in f if move[1]) for f in found if any(d for _, d in f)]


def kernel(
    n, sv, mat_hbm, table_hbm, ids_hbm, out, coarse,
    raw, mat, table, ids, vec, halo, coef, cond, cond_out, cond_in, id_out, id_in,
    edge_out, edge_in, aug, rows, halves, squares, sums, sums_in,
    load_sem, send_sem, recv_sem, small_send, small_recv, ar_send, ar_recv, token,
):
    me = lax.axis_index("slab")
    right, left = lax.rem(me + 1, n), lax.rem(me + n - 1, n)
    sides = (left, right)

    def moved(moves):
        dev = me
        for (stride, size), d in moves:
            pos = lax.rem(lax.div(me, stride), size)
            dev = dev + (lax.rem(pos + d, size) - pos) * stride
        return dev

    def signal(sem, dev):
        pl.semaphore_signal(sem, inc=1, device_id=(dev,), device_id_type=pl.DeviceIdType.MESH)

    def remote(src, dst, ssem, rsem, dev):
        return pltpu.make_async_remote_copy(
            src_ref=src, dst_ref=dst, send_sem=ssem, recv_sem=rsem,
            device_id=(dev,), device_id_type=pl.DeviceIdType.MESH,
        )

    barrier = pltpu.get_barrier_semaphore()
    known = [left, right] + [moved((move,)) for move in ENTRY]
    for dev in known:
        signal(barrier, dev)

    first = [
        pltpu.make_async_copy(mat_hbm, mat, load_sem.at[0]),
        pltpu.make_async_copy(table_hbm, table, load_sem.at[1]),
        pltpu.make_async_copy(ids_hbm, ids, load_sem.at[2]),
    ]
    part = GROUP * PLANE // 128 * PLANES
    loads = [
        pltpu.make_async_copy(sv.at[pl.ds(q * part, part)], raw.at[pl.ds(q * part, part)], load_sem.at[3 + q])
        for q in range(GROUPS)
    ]
    for c in first + loads:
        c.start()
    for c in first:
        c.wait()

    for z in range(PLANES):
        for y in range(NY):
            cols = slice(y * NX, (y + 1) * NX)
            m = jnp.broadcast_to(mat[z : z + 1, cols], (8, NX))
            k = jnp.zeros((8, NX), jnp.float32)
            for j in range(NMAT):
                k = jnp.where(m == j, table[j], k)
            cond[z, :, cols] = k
            cond_out[z, :, cols] = k[0:1]
    id_out[0] = jnp.full((8, 128), ids[0], jnp.int32)
    id_out[1] = jnp.full((8, 128), ids[BLOCKS - 1], jnp.int32)

    for q in range(GROUPS):
        loads[q].wait()
        for z in range(PLANES):
            for t in range(PLANE // 128):
                vec[0, z, q * GROUP : (q + 1) * GROUP, t * 128 : (t + 1) * 128] = raw[
                    pl.ds(q * part + t * PLANES + z, GROUP, stride=PLANE // 128 * PLANES), :
                ]

    pl.semaphore_wait(barrier, len(known))

    small = []
    for z in range(PLANES):
        small.append(remote(cond_out.at[z], cond_in.at[1 - z], small_send.at[z], small_recv.at[z], sides[z]))
        small.append(remote(id_out.at[z], id_in.at[1 - z], small_send.at[2 + z], small_recv.at[2 + z], sides[z]))
    for c in small:
        c.start()

    def plane_copy(s, q, z):
        lanes = pl.ds(pl.multiple_of(q * GROUP, GROUP), GROUP)
        return remote(
            vec.at[s, z, lanes], halo.at[s, 1 - z, lanes],
            send_sem.at[s, q, z], recv_sem.at[s, q, z], sides[z],
        )

    for q in range(GROUPS):
        for z in range(PLANES):
            plane_copy(0, q, z).start()

    def pass_token(turn):
        for i, move in enumerate(TOKENS[turn]):
            signal(token.at[turn, i], moved((move,)))

    def take_token(turn):
        for i in range(len(TOKENS[turn])):
            pl.semaphore_wait(token.at[turn, i], 1)

    pass_token(0)

    for c in small:
        c.wait_recv()

    has_below = (me > 0).astype(jnp.float32)
    has_above = (me < n - 1).astype(jnp.float32)
    xpos = lax.broadcasted_iota(jnp.int32, (8, NX), 1)
    west_ok, east_ok = xpos > 0, xpos < NX - 1

    def face(k, other):
        return 2.0 * k * other / (k + other)

    for z in range(PLANES):
        for y in range(NY):
            cols = slice(y * NX, (y + 1) * NX)
            k = cond[z, :, cols]
            zero = jnp.zeros_like(k)
            fw = face(k, pltpu.roll(k, 1, axis=1))
            fe = face(k, pltpu.roll(k, NX - 1, axis=1))
            fs = face(k, cond[z, :, (y - 1) * NX : y * NX]) if y > 0 else k
            fn = face(k, cond[z, :, (y + 1) * NX : (y + 2) * NX]) if y < NY - 1 else k
            below = cond[0, :, cols] if z == 1 else jnp.broadcast_to(cond_in[0, :, cols], (8, NX))
            above = cond[1, :, cols] if z == 0 else jnp.broadcast_to(cond_in[1, :, cols], (8, NX))
            fd, fu = face(k, below), face(k, above)
            hd = has_below if z == 0 else 1.0
            hu = has_above if z == 1 else 1.0
            dsum = (
                jnp.where(west_ok, fw, k) + jnp.where(east_ok, fe, k) + fs + fn
                + (hd * fd + (1.0 - hd) * k) + (hu * fu + (1.0 - hu) * k)
            )
            scale = WEIGHT / dsum
            coef[z, 0, :, cols] = jnp.where(west_ok, fw * scale, zero)
            coef[z, 1, :, cols] = jnp.where(east_ok, fe * scale, zero)
            coef[z, 2, :, cols] = fs * scale
            coef[z, 3, :, cols] = fn * scale
            coef[z, 4, :, cols] = fd * scale * hd
            coef[z, 5, :, cols] = fu * scale * hu

    def sweep(t, carry):
        s, q = lax.div(t, GROUPS), lax.rem(t, GROUPS)
        lanes = pl.ds(pl.multiple_of(q * GROUP, GROUP), GROUP)
        for z in range(PLANES):
            plane_copy(s, q, z).wait_recv()
        square = jnp.zeros((GROUP, NX), jnp.float32)
        for z in range(PLANES):
            for y in range(NY):
                cols = slice(y * NX, (y + 1) * NX)
                c = vec[s, z, lanes, cols]
                acc = c * (1.0 - WEIGHT)
                acc += coef[z, 0, :, cols] * pltpu.roll(c, 1, axis=1)
                acc += coef[z, 1, :, cols] * pltpu.roll(c, NX - 1, axis=1)
                if y > 0:
                    acc += coef[z, 2, :, cols] * vec[s, z, lanes, (y - 1) * NX : y * NX]
                if y < NY - 1:
                    acc += coef[z, 3, :, cols] * vec[s, z, lanes, (y + 1) * NX : (y + 2) * NX]
                below = vec[s, 0, lanes, cols] if z == 1 else halo[s, 0, lanes, cols]
                above = vec[s, 1, lanes, cols] if z == 0 else halo[s, 1, lanes, cols]
                acc += coef[z, 4, :, cols] * below
                acc += coef[z, 5, :, cols] * above
                vec[s + 1, z, lanes, cols] = acc
                square += acc * acc

            @pl.when(s < SWEEPS - 1)
            def _():
                plane_copy(s + 1, q, z).start()

        squares[lanes, :] = square[:, 0:128] + square[:, 128:NX]
        return carry

    lax.fori_loop(0, GROUPS, sweep, 0)
    take_token(0)
    pass_token(1)
    lax.fori_loop(GROUPS, 2 * GROUPS, sweep, 0)
    take_token(1)
    pass_token(2)
    lax.fori_loop(2 * GROUPS, SWEEPS * GROUPS, sweep, 0)
    take_token(2)

    i_pos = lax.broadcasted_iota(jnp.int32, (K, 128), 0)
    j_pos = lax.broadcasted_iota(jnp.int32, (K, 128), 1)
    each = jnp.sum(squares[...], axis=1, keepdims=True)
    row = jnp.sum(jnp.where(i_pos == j_pos, each, 0.0), axis=0, keepdims=True)
    sums[0] = jnp.broadcast_to(row, (8, 128))

    groups = [peers(step) for step in STEPS]
    slot0 = [sum(len(g) for g in groups[:step]) for step in range(len(STEPS))]

    def reduce_copy(step, d):
        slot = slot0[step] + d
        return remote(sums.at[step], sums_in.at[slot], ar_send.at[slot], ar_recv.at[slot], moved(groups[step][d]))

    def reduce_send(step):
        for d in range(len(groups[step])):
            reduce_copy(step, d).start()

    def reduce_recv(step):
        tot = sums[step]
        for d in range(len(groups[step])):
            reduce_copy(step, d).wait_recv()
            tot = tot + sums_in[slot0[step] + d]
        sums[step + 1] = tot

    reduce_send(0)

    nt = (((1,), (1,)), ((), ()))
    dot = functools.partial(lax.dot_general, preferred_element_type=jnp.float32)
    local = []
    for b in range(BLOCKS):
        z, c = divmod(b, PLANE // BLKR)
        v = vec[SWEEPS, z, :, c * BLKR : (c + 1) * BLKR] * LIFT
        hi = v.astype(jnp.bfloat16)
        lo = (v - hi.astype(jnp.float32)).astype(jnp.bfloat16)
        halves[b, 0:K] = hi
        halves[b, K : 2 * K] = lo
        g = dot(hi, hi, nt) + dot(hi, lo, nt) + dot(lo, hi, nt)
        local.append(g * (1.0 / BLKR))
        if b == BLOCKS // 2 - 1:
            reduce_recv(0)
            reduce_send(1)

    same = [None] + [(ids[b] == ids[b - 1]).astype(jnp.float32) for b in range(1, BLOCKS)]
    run = [local[0]]
    for b in range(1, BLOCKS):
        run.append(local[b] + same[b] * run[b - 1])
    for b in range(BLOCKS - 2, -1, -1):
        run[b] = run[b] + same[b + 1] * (run[b + 1] - run[b])
    edge_out[0] = run[0]
    edge_out[1] = run[BLOCKS - 1]
    edges = [remote(edge_out.at[z], edge_in.at[1 - z], small_send.at[4 + z], small_recv.at[4 + z], sides[z]) for z in range(PLANES)]
    for c in edges:
        c.start()

    for c in edges:
        c.wait_recv()
    pad = jnp.zeros((K, 2 * K), jnp.float32)
    end = jnp.zeros((K, K), jnp.float32)
    for b in range(BLOCKS):
        from_left = jnp.where(id_in[0, 0:1, 0:K] == ids[b], 1.0, 0.0) * has_below
        from_right = jnp.where(id_in[1, 0:1, 0:K] == ids[b], 1.0, 0.0) * has_above
        g = run[b] + from_left * edge_in[0] + from_right * edge_in[1]
        aug[pl.ds(b, K, stride=BLOCKS), :] = jnp.concatenate([pad, g, end], axis=1)

    reduce_recv(1)
    reduce_send(2)

    lane = lax.broadcasted_iota(jnp.int32, (BLOCKS, 128), 1)
    r = [
        aug[i * BLOCKS : (i + 1) * BLOCKS, :] + jnp.where((lane == i) | (lane == K + i), 1.0, 0.0)
        for i in range(K)
    ]
    for k in range(K):
        d = jnp.broadcast_to(r[k][:, 2 * K + k : 2 * K + k + 1], (BLOCKS, 128))
        scaled = r[k] / d
        for i in range(k + 1, K):
            r[i] = r[i] - jnp.broadcast_to(r[k][:, 2 * K + i : 2 * K + i + 1], (BLOCKS, 128)) * scaled
        keep = (lane < 2 * K) | (lane >= 2 * K + k)
        rows[k * BLOCKS : (k + 1) * BLOCKS, :] = jnp.where(keep, r[k] * lax.rsqrt(d), 0.0)

    for b in range(BLOCKS):
        z, c = divmod(b, PLANE // BLKR)
        w = rows[pl.ds(b, K, stride=BLOCKS), :][:, 0 : 2 * K]
        hi = w.astype(jnp.bfloat16)
        lo = (w - hi.astype(jnp.float32)).astype(jnp.bfloat16)
        nn = (((1,), (0,)), ((), ()))
        x = halves[b]
        p = dot(hi, x, nn) + dot(lo, x, nn)
        for t in range(BLKR // 128):
            out[pl.ds((c * (BLKR // 128) + t) * PLANES + z, K, stride=PLANE // 128 * PLANES), :] = p[:, t * 128 : (t + 1) * 128]

    reduce_recv(2)
    mean_sq = sums[len(STEPS)][0:1, 0:K] * (1.0 / CELLS)
    inv = lax.rsqrt(mean_sq + EPS) * (1.0 / LIFT)
    for b in range(BLOCKS):
        coarse[b] = rows[pl.ds(b, K, stride=BLOCKS), :][:, 2 * K : 3 * K] * inv

    for c in small + edges:
        c.wait_send()
    for step in range(len(STEPS)):
        for d in range(len(groups[step])):
            reduce_copy(step, d).wait_send()

    def drain(t, carry):
        for z in range(PLANES):
            plane_copy(lax.div(t, GROUPS), lax.rem(t, GROUPS), z).wait_send()
        return carry

    lax.fori_loop(0, SWEEPS * GROUPS, drain, 0)


def lines_of(vectors):
    return jnp.transpose(vectors.reshape(K, PLANES, PLANE // 128, 128), (0, 2, 1, 3)).reshape(-1, 128)


def local(n, start_vectors, materials, conduct_table, aggregate_ids):
    f32 = jnp.float32
    slots = sum(len(peers(step)) for step in STEPS)
    lines = K * PLANES * PLANE // 128
    vmem, anywhere = pl.BlockSpec(memory_space=pltpu.VMEM), pl.BlockSpec(memory_space=pl.ANY)
    out, coarse = pl.pallas_call(
        functools.partial(kernel, n),
        out_shape=(
            jax.ShapeDtypeStruct((lines, 128), f32),
            jax.ShapeDtypeStruct((BLOCKS, K, K), f32),
        ),
        in_specs=[anywhere] * 4,
        out_specs=(vmem, vmem),
        scratch_shapes=[
            pltpu.VMEM((lines, 128), f32),
            pltpu.VMEM((PLANES, PLANE), jnp.int32),
            pltpu.SMEM((NMAT,), f32),
            pltpu.SMEM((BLOCKS,), jnp.int32),
            pltpu.VMEM((SWEEPS + 1, PLANES, K, PLANE), f32),
            pltpu.VMEM((SWEEPS, 2, K, PLANE), f32),
            pltpu.VMEM((PLANES, 6, 8, PLANE), f32),
            pltpu.VMEM((PLANES, 8, PLANE), f32),
            pltpu.VMEM((PLANES, 1, PLANE), f32),
            pltpu.VMEM((2, 1, PLANE), f32),
            pltpu.VMEM((2, 8, 128), jnp.int32),
            pltpu.VMEM((2, 8, 128), jnp.int32),
            pltpu.VMEM((2, K, K), f32),
            pltpu.VMEM((2, K, K), f32),
            pltpu.VMEM((K * BLOCKS, 128), f32),
            pltpu.VMEM((K * BLOCKS, 128), f32),
            pltpu.VMEM((BLOCKS, 2 * K, BLKR), jnp.bfloat16),
            pltpu.VMEM((K, 128), f32),
            pltpu.VMEM((len(STEPS) + 1, 8, 128), f32),
            pltpu.VMEM((slots, 8, 128), f32),
            pltpu.SemaphoreType.DMA((3 + GROUPS,)),
            pltpu.SemaphoreType.DMA((SWEEPS, GROUPS, PLANES)),
            pltpu.SemaphoreType.DMA((SWEEPS, GROUPS, PLANES)),
            pltpu.SemaphoreType.DMA((6,)),
            pltpu.SemaphoreType.DMA((6,)),
            pltpu.SemaphoreType.DMA((slots,)),
            pltpu.SemaphoreType.DMA((slots,)),
            pltpu.SemaphoreType.REGULAR((len(TOKENS), len(ENTRY))),
        ],
        compiler_params=pltpu.CompilerParams(
            collective_id=0, has_side_effects=True, vmem_limit_bytes=40 * 2**20
        ),
        name="adaptive_setup",
    )(lines_of(start_vectors), materials, conduct_table, aggregate_ids)
    out = jnp.transpose(out.reshape(K, PLANE // 128, PLANES, 128), (0, 2, 1, 3)).reshape(K, PLANES, PLANE)
    return out, coarse


def solution(mesh):
    n = mesh.shape["slab"]
    return jax.shard_map(
        functools.partial(local, n),
        mesh=mesh,
        in_specs=(P(None, "slab", None), P("slab", None), P(), P("slab")),
        out_specs=(P(None, "slab", None), P("slab", None, None)),
        check_vma=False,
    )
```

```python
import functools

import jax
import jax.numpy as jnp
from jax import lax
from jax.experimental import pallas as pl
from jax.experimental.pallas import tpu as pltpu
from jax.sharding import PartitionSpec as P

K = 32
BLKR = 512
NX = 256
NY = 16
PLANE = NX * NY
SWEEPS = 4
NMAT = 8
GROUP = 8
GROUPS = K // GROUP
BLOCKS = 16
PLANES = 2
CELLS = 1024 * PLANE

WEIGHT = 2.0 / 3.0
EPS = 1e-06
LIFT = 2.0**20


CORE, X, Y, Z = (1, 2), (2, 4), (128, 4), (8, 16)
STEPS = ((CORE,), (X, Y), (Z,))
ENTRY = ((X, 1), (X, 3), (Y, 1), (Y, 3), (Z, 1), (Z, 15))
TOKENS = (ENTRY, ((X, 1), (X, 2), (X, 3), (Z, 2), (Z, 14)), ((Z, 4), (Z, 12)))


def peers(step):
    found = [()]
    for axis in step:
        found = [f + ((axis, d),) for f in found for d in range(axis[1])]
    return [tuple(move for move in f if move[1]) for f in found if any(d for _, d in f)]


def kernel(
    n, sv, mat_hbm, table_hbm, ids_hbm, out, rows, total,
    raw, mat, table, ids, vec, halo, coef, cond, cond_out, cond_in, id_out, id_in,
    edge_out, edge_in, aug, halves, squares, sums, sums_in,
    load_sem, send_sem, recv_sem, small_send, small_recv, ar_send, ar_recv, token,
):
    me = lax.axis_index("slab")
    right, left = lax.rem(me + 1, n), lax.rem(me + n - 1, n)
    sides = (left, right)
    to_ok = (me > 0, me < n - 1)
    from_ok = (me < n - 1, me > 0)

    def moved(moves):
        dev = me
        for (stride, size), d in moves:
            pos = lax.rem(lax.div(me, stride), size)
            dev = dev + (lax.rem(pos + d, size) - pos) * stride
        return dev

    def signal(sem, dev):
        pl.semaphore_signal(sem, inc=1, device_id=(dev,), device_id_type=pl.DeviceIdType.MESH)

    def remote(src, dst, ssem, rsem, dev):
        return pltpu.make_async_remote_copy(
            src_ref=src, dst_ref=dst, send_sem=ssem, recv_sem=rsem,
            device_id=(dev,), device_id_type=pl.DeviceIdType.MESH,
        )

    barrier = pltpu.get_barrier_semaphore()
    for move in ENTRY:
        signal(barrier, moved((move,)))
    for z in range(PLANES):

        @pl.when(to_ok[z])
        def _():
            signal(barrier, sides[z])

    entries = len(ENTRY) + to_ok[0].astype(jnp.int32) + to_ok[1].astype(jnp.int32)

    first = [
        pltpu.make_async_copy(mat_hbm, mat, load_sem.at[0]),
        pltpu.make_async_copy(table_hbm, table, load_sem.at[1]),
        pltpu.make_async_copy(ids_hbm, ids, load_sem.at[2]),
    ]
    part = GROUP * PLANE // 128 * PLANES
    loads = [
        pltpu.make_async_copy(sv.at[pl.ds(q * part, part)], raw.at[pl.ds(q * part, part)], load_sem.at[3 + q])
        for q in range(GROUPS)
    ]
    for c in first + loads:
        c.start()
    for c in first:
        c.wait()

    for z in range(PLANES):
        for y in range(NY):
            cols = slice(y * NX, (y + 1) * NX)
            m = jnp.broadcast_to(mat[z : z + 1, cols], (8, NX))
            k = jnp.zeros((8, NX), jnp.float32)
            for j in range(NMAT):
                k = jnp.where(m == j, table[j], k)
            cond[z, :, cols] = k
            cond_out[z, :, cols] = k[0:1]
    id_out[0] = jnp.full((8, 128), ids[0], jnp.int32)
    id_out[1] = jnp.full((8, 128), ids[BLOCKS - 1], jnp.int32)

    pl.semaphore_wait(barrier, entries)

    def send(z, copy):
        @pl.when(to_ok[z])
        def _():
            copy().start()

    def sent(z, copy):
        @pl.when(to_ok[z])
        def _():
            copy().wait_send()

    def received(z, copy):
        @pl.when(from_ok[z])
        def _():
            copy().wait_recv()


    def small_copy(z, i):
        src, dst = ((cond_out, cond_in), (id_out, id_in), (edge_out, edge_in))[i]
        return remote(src.at[z], dst.at[1 - z], small_send.at[i, z], small_recv.at[i, z], sides[z])

    for i in range(2):
        for z in range(PLANES):
            send(z, functools.partial(small_copy, z, i))

    def plane_copy(s, q, z):
        lanes = pl.ds(pl.multiple_of(q * GROUP, GROUP), GROUP)
        return remote(
            vec.at[s, z, lanes], halo.at[s, 1 - z, lanes],
            send_sem.at[s, q, z], recv_sem.at[s, q, z], sides[z],
        )

    for q in range(GROUPS):
        loads[q].wait()
        for z in range(PLANES):
            for t in range(PLANE // 128):
                vec[0, z, q * GROUP : (q + 1) * GROUP, t * 128 : (t + 1) * 128] = raw[
                    pl.ds(q * part + t * PLANES + z, GROUP, stride=PLANE // 128 * PLANES), :
                ]
            send(z, functools.partial(plane_copy, 0, q, z))

    def pass_token(turn):
        for i, move in enumerate(TOKENS[turn]):
            signal(token.at[turn, i], moved((move,)))

    def take_token(turn):
        for i in range(len(TOKENS[turn])):
            pl.semaphore_wait(token.at[turn, i], 1)

    pass_token(0)

    for z in range(PLANES):

        @pl.when(jnp.logical_not(from_ok[z]))
        def _():
            cond_in[1 - z] = jnp.zeros((1, PLANE), jnp.float32)
            id_in[1 - z] = jnp.zeros((8, 128), jnp.int32)
            edge_in[1 - z] = jnp.zeros((K, K), jnp.float32)

            def clear(t, carry):
                s, q = lax.div(t, GROUPS), lax.rem(t, GROUPS)
                lanes = pl.ds(pl.multiple_of(q * GROUP, GROUP), GROUP)
                halo[s, 1 - z, lanes] = jnp.zeros((GROUP, PLANE), jnp.float32)
                return carry

            lax.fori_loop(0, SWEEPS * GROUPS, clear, 0)

    for i in range(2):
        for z in range(PLANES):
            received(z, functools.partial(small_copy, z, i))

    has_below = (me > 0).astype(jnp.float32)
    has_above = (me < n - 1).astype(jnp.float32)
    xpos = lax.broadcasted_iota(jnp.int32, (8, NX), 1)
    west_ok, east_ok = xpos > 0, xpos < NX - 1

    def face(k, other):
        return 2.0 * k * other / (k + other)

    for z in range(PLANES):
        for y in range(NY):
            cols = slice(y * NX, (y + 1) * NX)
            k = cond[z, :, cols]
            zero = jnp.zeros_like(k)
            fw = face(k, pltpu.roll(k, 1, axis=1))
            fe = face(k, pltpu.roll(k, NX - 1, axis=1))
            fs = face(k, cond[z, :, (y - 1) * NX : y * NX]) if y > 0 else k
            fn = face(k, cond[z, :, (y + 1) * NX : (y + 2) * NX]) if y < NY - 1 else k
            below = cond[0, :, cols] if z == 1 else jnp.broadcast_to(cond_in[0, :, cols], (8, NX))
            above = cond[1, :, cols] if z == 0 else jnp.broadcast_to(cond_in[1, :, cols], (8, NX))
            fd, fu = face(k, below), face(k, above)
            hd = has_below if z == 0 else 1.0
            hu = has_above if z == 1 else 1.0
            dsum = (
                jnp.where(west_ok, fw, k) + jnp.where(east_ok, fe, k) + fs + fn
                + (hd * fd + (1.0 - hd) * k) + (hu * fu + (1.0 - hu) * k)
            )
            scale = WEIGHT / dsum
            coef[z, 0, :, cols] = jnp.where(west_ok, fw * scale, zero)
            coef[z, 1, :, cols] = jnp.where(east_ok, fe * scale, zero)
            coef[z, 2, :, cols] = fs * scale
            coef[z, 3, :, cols] = fn * scale
            coef[z, 4, :, cols] = fd * scale * hd
            coef[z, 5, :, cols] = fu * scale * hu

    def sweep(t, carry):
        s, q = lax.div(t, GROUPS), lax.rem(t, GROUPS)
        lanes = pl.ds(pl.multiple_of(q * GROUP, GROUP), GROUP)
        for z in range(PLANES):
            received(z, functools.partial(plane_copy, s, q, z))
        square = jnp.zeros((GROUP, NX), jnp.float32)
        for z in range(PLANES):
            for y in range(NY):
                cols = slice(y * NX, (y + 1) * NX)
                c = vec[s, z, lanes, cols]
                acc = c * (1.0 - WEIGHT)
                acc += coef[z, 0, :, cols] * pltpu.roll(c, 1, axis=1)
                acc += coef[z, 1, :, cols] * pltpu.roll(c, NX - 1, axis=1)
                if y > 0:
                    acc += coef[z, 2, :, cols] * vec[s, z, lanes, (y - 1) * NX : y * NX]
                if y < NY - 1:
                    acc += coef[z, 3, :, cols] * vec[s, z, lanes, (y + 1) * NX : (y + 2) * NX]
                below = vec[s, 0, lanes, cols] if z == 1 else halo[s, 0, lanes, cols]
                above = vec[s, 1, lanes, cols] if z == 0 else halo[s, 1, lanes, cols]
                acc += coef[z, 4, :, cols] * below
                acc += coef[z, 5, :, cols] * above
                vec[s + 1, z, lanes, cols] = acc
                square += acc * acc

            @pl.when((s < SWEEPS - 1) & to_ok[z])
            def _():
                plane_copy(s + 1, q, z).start()

        squares[lanes, :] = square[:, 0:128] + square[:, 128:NX]
        return carry

    lax.fori_loop(0, GROUPS, sweep, 0)
    take_token(0)
    pass_token(1)
    lax.fori_loop(GROUPS, 2 * GROUPS, sweep, 0)
    take_token(1)
    pass_token(2)
    lax.fori_loop(2 * GROUPS, SWEEPS * GROUPS, sweep, 0)
    take_token(2)

    i_pos = lax.broadcasted_iota(jnp.int32, (K, 128), 0)
    j_pos = lax.broadcasted_iota(jnp.int32, (K, 128), 1)
    each = jnp.sum(squares[...], axis=1, keepdims=True)
    row = jnp.sum(jnp.where(i_pos == j_pos, each, 0.0), axis=0, keepdims=True)
    sums[0] = row

    groups = [peers(step) for step in STEPS]
    slot0 = [sum(len(g) for g in groups[:step]) for step in range(len(STEPS))]

    def reduce_copy(step, d):
        slot = slot0[step] + d
        return remote(sums.at[step], sums_in.at[slot], ar_send.at[slot], ar_recv.at[slot], moved(groups[step][d]))

    def reduce_send(step):
        for d in range(len(groups[step])):
            reduce_copy(step, d).start()

    def reduce_recv(step):
        tot = sums[step]
        for d in range(len(groups[step])):
            reduce_copy(step, d).wait_recv()
            tot = tot + sums_in[slot0[step] + d]
        return tot

    reduce_send(0)

    nt = (((1,), (1,)), ((), ()))
    dot = functools.partial(lax.dot_general, preferred_element_type=jnp.float32)
    local = []
    for b in range(BLOCKS):
        z, c = divmod(b, PLANE // BLKR)
        v = vec[SWEEPS, z, :, c * BLKR : (c + 1) * BLKR] * LIFT
        hi = v.astype(jnp.bfloat16)
        lo = (v - hi.astype(jnp.float32)).astype(jnp.bfloat16)
        halves[b, 0:K] = hi
        halves[b, K : 2 * K] = lo
        g = dot(hi, hi, nt) + dot(hi, lo, nt) + dot(lo, hi, nt)
        local.append(g * (1.0 / BLKR))
        if b == BLOCKS // 2 - 1:
            sums[1] = reduce_recv(0)
            reduce_send(1)

    same = [None] + [(ids[b] == ids[b - 1]).astype(jnp.float32) for b in range(1, BLOCKS)]
    run = [local[0]]
    for b in range(1, BLOCKS):
        run.append(local[b] + same[b] * run[b - 1])
    for b in range(BLOCKS - 2, -1, -1):
        run[b] = run[b] + same[b + 1] * (run[b + 1] - run[b])
    edge_out[0] = run[0]
    edge_out[1] = run[BLOCKS - 1]
    for z in range(PLANES):
        send(z, functools.partial(small_copy, z, 2))

    for z in range(PLANES):
        received(z, functools.partial(small_copy, z, 2))
    pad = jnp.zeros((K, 2 * K), jnp.float32)
    end = jnp.zeros((K, K), jnp.float32)
    for b in range(BLOCKS):
        from_left = jnp.where(id_in[0, 0:1, 0:K] == ids[b], 1.0, 0.0) * has_below
        from_right = jnp.where(id_in[1, 0:1, 0:K] == ids[b], 1.0, 0.0) * has_above
        g = run[b] + from_left * edge_in[0] + from_right * edge_in[1]
        aug[pl.ds(b, K, stride=BLOCKS), :] = jnp.concatenate([pad, g, end], axis=1)

    sums[2] = reduce_recv(1)
    reduce_send(2)

    lane = lax.broadcasted_iota(jnp.int32, (BLOCKS, 128), 1)
    r = [
        aug[i * BLOCKS : (i + 1) * BLOCKS, :] + jnp.where((lane == i) | (lane == K + i), 1.0, 0.0)
        for i in range(K)
    ]
    for k in range(K):
        d = jnp.broadcast_to(r[k][:, 2 * K + k : 2 * K + k + 1], (BLOCKS, 128))
        scaled = r[k] / d
        for i in range(k + 1, K):
            r[i] = r[i] - jnp.broadcast_to(r[k][:, 2 * K + i : 2 * K + i + 1], (BLOCKS, 128)) * scaled
        keep = (lane < 2 * K) | (lane >= 2 * K + k)
        rows[k * BLOCKS : (k + 1) * BLOCKS, :] = jnp.where(keep, r[k] * lax.rsqrt(d), 0.0)

    for b in range(BLOCKS):
        z, c = divmod(b, PLANE // BLKR)
        w = rows[pl.ds(b, K, stride=BLOCKS), :][:, 0 : 2 * K]
        hi = w.astype(jnp.bfloat16)
        lo = (w - hi.astype(jnp.float32)).astype(jnp.bfloat16)
        nn = (((1,), (0,)), ((), ()))
        x = halves[b]
        p = dot(hi, x, nn) + dot(lo, x, nn)
        for t in range(BLKR // 128):
            out[pl.ds((c * (BLKR // 128) + t) * PLANES + z, K, stride=PLANE // 128 * PLANES), :] = p[:, t * 128 : (t + 1) * 128]

    total[...] = reduce_recv(2)

    for i in range(3):
        for z in range(PLANES):
            sent(z, functools.partial(small_copy, z, i))
    for step in range(len(STEPS)):
        for d in range(len(groups[step])):
            reduce_copy(step, d).wait_send()

    def drain(t, carry):
        for z in range(PLANES):
            sent(z, functools.partial(plane_copy, lax.div(t, GROUPS), lax.rem(t, GROUPS), z))
        return carry

    lax.fori_loop(0, SWEEPS * GROUPS, drain, 0)


def finish(found, rows_in, total_in, out, coarse, rows, total, scaled, sem):
    large = pltpu.make_async_copy(found, out, sem.at[0])
    parts = [pltpu.make_async_copy(rows_in, rows, sem.at[2]), pltpu.make_async_copy(total_in, total, sem.at[3])]
    for c in parts + [large]:
        c.start()
    for c in parts:
        c.wait()
    inv = lax.rsqrt(total[0:1, 0:K] * (1.0 / CELLS) + EPS) * (1.0 / LIFT)
    for b in range(BLOCKS):
        scaled[b] = rows[pl.ds(b, K, stride=BLOCKS), :][:, 2 * K : 3 * K] * inv
    small = pltpu.make_async_copy(scaled, coarse, sem.at[1])
    small.start()
    large.wait()
    small.wait()


def lines_of(vectors):
    return jnp.transpose(vectors.reshape(K, PLANES, PLANE // 128, 128), (0, 2, 1, 3)).reshape(-1, 128)


def local(n, start_vectors, materials, conduct_table, aggregate_ids):
    f32 = jnp.float32
    slots = sum(len(peers(step)) for step in STEPS)
    lines = K * PLANES * PLANE // 128
    vmem, anywhere = pl.BlockSpec(memory_space=pltpu.VMEM), pl.BlockSpec(memory_space=pl.ANY)
    found, rows, total = pl.pallas_call(
        functools.partial(kernel, n),
        out_shape=(
            jax.ShapeDtypeStruct((lines, 128), f32),
            jax.ShapeDtypeStruct((K * BLOCKS, 128), f32),
            jax.ShapeDtypeStruct((1, 128), f32),
        ),
        in_specs=[anywhere] * 4,
        out_specs=(vmem, vmem, vmem),
        scratch_shapes=[
            pltpu.VMEM((lines, 128), f32),
            pltpu.VMEM((PLANES, PLANE), jnp.int32),
            pltpu.SMEM((NMAT,), f32),
            pltpu.SMEM((BLOCKS,), jnp.int32),
            pltpu.VMEM((SWEEPS + 1, PLANES, K, PLANE), f32),
            pltpu.VMEM((SWEEPS, 2, K, PLANE), f32),
            pltpu.VMEM((PLANES, 6, 8, PLANE), f32),
            pltpu.VMEM((PLANES, 8, PLANE), f32),
            pltpu.VMEM((PLANES, 1, PLANE), f32),
            pltpu.VMEM((2, 1, PLANE), f32),
            pltpu.VMEM((2, 8, 128), jnp.int32),
            pltpu.VMEM((2, 8, 128), jnp.int32),
            pltpu.VMEM((2, K, K), f32),
            pltpu.VMEM((2, K, K), f32),
            pltpu.VMEM((K * BLOCKS, 128), f32),
            pltpu.VMEM((BLOCKS, 2 * K, BLKR), jnp.bfloat16),
            pltpu.VMEM((K, 128), f32),
            pltpu.VMEM((len(STEPS), 1, 128), f32),
            pltpu.VMEM((slots, 1, 128), f32),
            pltpu.SemaphoreType.DMA((3 + GROUPS,)),
            pltpu.SemaphoreType.DMA((SWEEPS, GROUPS, PLANES)),
            pltpu.SemaphoreType.DMA((SWEEPS, GROUPS, PLANES)),
            pltpu.SemaphoreType.DMA((3, PLANES)),
            pltpu.SemaphoreType.DMA((3, PLANES)),
            pltpu.SemaphoreType.DMA((slots,)),
            pltpu.SemaphoreType.DMA((slots,)),
            pltpu.SemaphoreType.REGULAR((len(TOKENS), len(ENTRY))),
        ],
        compiler_params=pltpu.CompilerParams(
            collective_id=0, has_side_effects=True, vmem_limit_bytes=54840524
        ),
        name="adaptive_setup",
    )(lines_of(start_vectors), materials, conduct_table, aggregate_ids)
    out, coarse = pl.pallas_call(
        finish,
        out_shape=(jax.ShapeDtypeStruct((lines, 128), f32), jax.ShapeDtypeStruct((BLOCKS, K, K), f32)),
        in_specs=[anywhere] * 3,
        out_specs=(anywhere, anywhere),
        scratch_shapes=[
            pltpu.VMEM((K * BLOCKS, 128), f32),
            pltpu.VMEM((1, 128), f32),
            pltpu.VMEM((BLOCKS, K, K), f32),
            pltpu.SemaphoreType.DMA((4,)),
        ],
        compiler_params=pltpu.CompilerParams(vmem_limit_bytes=2 * 2**20),
        name="adaptive_finish",
    )(found, rows, total)
    out = jnp.transpose(out.reshape(K, PLANE // 128, PLANES, 128), (0, 2, 1, 3)).reshape(K, PLANES, PLANE)
    return out, coarse


def solution(mesh):
    n = mesh.shape["slab"]
    return jax.shard_map(
        functools.partial(local, n),
        mesh=mesh,
        in_specs=(P(None, "slab", None), P("slab", None), P(), P("slab")),
        out_specs=(P(None, "slab", None), P("slab", None, None)),
        check_vma=False,
    )
```

```python
import functools

import jax
import jax.numpy as jnp
from jax import lax
from jax.experimental import pallas as pl
from jax.experimental.pallas import tpu as pltpu
from jax.sharding import PartitionSpec as P

K = 32
BLKR = 512
NX = 256
NY = 16
PLANE = NX * NY
SWEEPS = 4
NMAT = 8
GROUP = 8
GROUPS = K // GROUP
BLOCKS = 16
PLANES = 2
CELLS = 1024 * PLANE

WEIGHT = 2.0 / 3.0
EPS = 1e-06
LIFT = 2.0**20


CORE, X, Y, Z = (1, 2), (2, 4), (128, 4), (8, 16)
STEPS = ((CORE,), (X, Y), (Z,))
ENTRY = ((X, 1), (X, 3), (Y, 1), (Y, 3), (Z, 1), (Z, 15))
TOKENS = (ENTRY, ((X, 1), (X, 2), (X, 3), (Z, 2), (Z, 14)), ((Z, 4), (Z, 12)))


def peers(step):
    found = [()]
    for axis in step:
        found = [f + ((axis, d),) for f in found for d in range(axis[1])]
    found.sort(key=lambda f: -sum(min(d, size - d) for (_, size), d in f))
    return [tuple(move for move in f if move[1]) for f in found if any(d for _, d in f)]


def kernel(
    n, sv, mat_hbm, table_hbm, ids_hbm, out, rows, total,
    raw, mat, table, ids, vec, halo, coef, cond, cond_out, cond_in, id_out, id_in,
    edge_out, edge_in, aug, halves, squares, sums, sums_in,
    load_sem, send_sem, recv_sem, small_send, small_recv, ar_send, ar_recv, token,
):
    me = lax.axis_index("slab")
    right, left = lax.rem(me + 1, n), lax.rem(me + n - 1, n)
    sides = (left, right)
    to_ok = (me > 0, me < n - 1)
    from_ok = (me < n - 1, me > 0)

    def moved(moves):
        dev = me
        for (stride, size), d in moves:
            pos = lax.rem(lax.div(me, stride), size)
            dev = dev + (lax.rem(pos + d, size) - pos) * stride
        return dev

    def signal(sem, dev):
        pl.semaphore_signal(sem, inc=1, device_id=(dev,), device_id_type=pl.DeviceIdType.MESH)

    def remote(src, dst, ssem, rsem, dev):
        return pltpu.make_async_remote_copy(
            src_ref=src, dst_ref=dst, send_sem=ssem, recv_sem=rsem,
            device_id=(dev,), device_id_type=pl.DeviceIdType.MESH,
        )

    barrier = pltpu.get_barrier_semaphore()
    for move in ENTRY:
        signal(barrier, moved((move,)))
    for z in range(PLANES):

        @pl.when(to_ok[z])
        def _():
            signal(barrier, sides[z])

    entries = len(ENTRY) + to_ok[0].astype(jnp.int32) + to_ok[1].astype(jnp.int32)

    first = [
        pltpu.make_async_copy(mat_hbm, mat, load_sem.at[0]),
        pltpu.make_async_copy(table_hbm, table, load_sem.at[1]),
        pltpu.make_async_copy(ids_hbm, ids, load_sem.at[2]),
    ]
    part = GROUP * PLANE // 128 * PLANES
    loads = [
        pltpu.make_async_copy(sv.at[pl.ds(q * part, part)], raw.at[pl.ds(q * part, part)], load_sem.at[3 + q])
        for q in range(GROUPS)
    ]
    for c in first + loads:
        c.start()
    for c in first:
        c.wait()

    for z in range(PLANES):
        for y in range(NY):
            cols = slice(y * NX, (y + 1) * NX)
            m = jnp.broadcast_to(mat[z : z + 1, cols], (8, NX))
            k = jnp.zeros((8, NX), jnp.float32)
            for j in range(NMAT):
                k = jnp.where(m == j, table[j], k)
            cond[z, :, cols] = k
            cond_out[z, :, cols] = k[0:1]
    id_out[0] = jnp.full((8, 128), ids[0], jnp.int32)
    id_out[1] = jnp.full((8, 128), ids[BLOCKS - 1], jnp.int32)

    pl.semaphore_wait(barrier, entries)

    def send(z, copy):
        @pl.when(to_ok[z])
        def _():
            copy().start()

    def sent(z, copy):
        @pl.when(to_ok[z])
        def _():
            copy().wait_send()

    def received(z, copy):
        @pl.when(from_ok[z])
        def _():
            copy().wait_recv()


    def small_copy(z, i):
        src, dst = ((cond_out, cond_in), (id_out, id_in), (edge_out, edge_in))[i]
        return remote(src.at[z], dst.at[1 - z], small_send.at[i, z], small_recv.at[i, z], sides[z])

    for i in range(2):
        for z in range(PLANES):
            send(z, functools.partial(small_copy, z, i))

    def plane_copy(s, q, z):
        lanes = pl.ds(pl.multiple_of(q * GROUP, GROUP), GROUP)
        return remote(
            vec.at[s, z, lanes], halo.at[s, 1 - z, lanes],
            send_sem.at[s, q, z], recv_sem.at[s, q, z], sides[z],
        )

    for q in range(GROUPS):
        loads[q].wait()
        for z in range(PLANES):
            for t in range(PLANE // 128):
                vec[0, z, q * GROUP : (q + 1) * GROUP, t * 128 : (t + 1) * 128] = raw[
                    pl.ds(q * part + t * PLANES + z, GROUP, stride=PLANE // 128 * PLANES), :
                ]
            send(z, functools.partial(plane_copy, 0, q, z))

    def pass_token(turn):
        for i, move in enumerate(TOKENS[turn]):
            signal(token.at[turn, i], moved((move,)))

    def take_token(turn):
        for i in range(len(TOKENS[turn])):
            pl.semaphore_wait(token.at[turn, i], 1)

    pass_token(0)

    for z in range(PLANES):

        @pl.when(jnp.logical_not(from_ok[z]))
        def _():
            cond_in[1 - z] = jnp.zeros((1, PLANE), jnp.float32)
            id_in[1 - z] = jnp.zeros((8, 128), jnp.int32)
            edge_in[1 - z] = jnp.zeros((K, K), jnp.float32)

            def clear(t, carry):
                s, q = lax.div(t, GROUPS), lax.rem(t, GROUPS)
                lanes = pl.ds(pl.multiple_of(q * GROUP, GROUP), GROUP)
                halo[s, 1 - z, lanes] = jnp.zeros((GROUP, PLANE), jnp.float32)
                return carry

            lax.fori_loop(0, SWEEPS * GROUPS, clear, 0)

    for i in range(2):
        for z in range(PLANES):
            received(z, functools.partial(small_copy, z, i))

    has_below = (me > 0).astype(jnp.float32)
    has_above = (me < n - 1).astype(jnp.float32)
    xpos = lax.broadcasted_iota(jnp.int32, (8, NX), 1)
    west_ok, east_ok = xpos > 0, xpos < NX - 1

    def face(k, other):
        return 2.0 * k * other / (k + other)

    for z in range(PLANES):
        for y in range(NY):
            cols = slice(y * NX, (y + 1) * NX)
            k = cond[z, :, cols]
            zero = jnp.zeros_like(k)
            fw = face(k, pltpu.roll(k, 1, axis=1))
            fe = face(k, pltpu.roll(k, NX - 1, axis=1))
            fs = face(k, cond[z, :, (y - 1) * NX : y * NX]) if y > 0 else k
            fn = face(k, cond[z, :, (y + 1) * NX : (y + 2) * NX]) if y < NY - 1 else k
            below = cond[0, :, cols] if z == 1 else jnp.broadcast_to(cond_in[0, :, cols], (8, NX))
            above = cond[1, :, cols] if z == 0 else jnp.broadcast_to(cond_in[1, :, cols], (8, NX))
            fd, fu = face(k, below), face(k, above)
            hd = has_below if z == 0 else 1.0
            hu = has_above if z == 1 else 1.0
            dsum = (
                jnp.where(west_ok, fw, k) + jnp.where(east_ok, fe, k) + fs + fn
                + (hd * fd + (1.0 - hd) * k) + (hu * fu + (1.0 - hu) * k)
            )
            scale = WEIGHT / dsum
            coef[z, 0, :, cols] = jnp.where(west_ok, fw * scale, zero)
            coef[z, 1, :, cols] = jnp.where(east_ok, fe * scale, zero)
            coef[z, 2, :, cols] = fs * scale
            coef[z, 3, :, cols] = fn * scale
            coef[z, 4, :, cols] = fd * scale * hd
            coef[z, 5, :, cols] = fu * scale * hu

    def sweep(t, carry):
        s, q = lax.div(t, GROUPS), lax.rem(t, GROUPS)
        lanes = pl.ds(pl.multiple_of(q * GROUP, GROUP), GROUP)
        for z in range(PLANES):
            received(z, functools.partial(plane_copy, s, q, z))
        square = jnp.zeros((GROUP, NX), jnp.float32)
        for z in range(PLANES):
            for y in range(NY):
                cols = slice(y * NX, (y + 1) * NX)
                c = vec[s, z, lanes, cols]
                acc = c * (1.0 - WEIGHT)
                acc += coef[z, 0, :, cols] * pltpu.roll(c, 1, axis=1)
                acc += coef[z, 1, :, cols] * pltpu.roll(c, NX - 1, axis=1)
                if y > 0:
                    acc += coef[z, 2, :, cols] * vec[s, z, lanes, (y - 1) * NX : y * NX]
                if y < NY - 1:
                    acc += coef[z, 3, :, cols] * vec[s, z, lanes, (y + 1) * NX : (y + 2) * NX]
                below = vec[s, 0, lanes, cols] if z == 1 else halo[s, 0, lanes, cols]
                above = vec[s, 1, lanes, cols] if z == 0 else halo[s, 1, lanes, cols]
                acc += coef[z, 4, :, cols] * below
                acc += coef[z, 5, :, cols] * above
                vec[s + 1, z, lanes, cols] = acc
                square += acc * acc

            @pl.when((s < SWEEPS - 1) & to_ok[z])
            def _():
                plane_copy(s + 1, q, z).start()

        squares[lanes, :] = square[:, 0:128] + square[:, 128:NX]
        return carry

    lax.fori_loop(0, GROUPS, sweep, 0)
    take_token(0)
    pass_token(1)
    lax.fori_loop(GROUPS, 2 * GROUPS, sweep, 0)
    take_token(1)
    pass_token(2)
    lax.fori_loop(2 * GROUPS, SWEEPS * GROUPS, sweep, 0)
    take_token(2)

    i_pos = lax.broadcasted_iota(jnp.int32, (K, 128), 0)
    j_pos = lax.broadcasted_iota(jnp.int32, (K, 128), 1)
    each = jnp.sum(squares[...], axis=1, keepdims=True)
    row = jnp.sum(jnp.where(i_pos == j_pos, each, 0.0), axis=0, keepdims=True)
    sums[0] = row

    groups = [peers(step) for step in STEPS]
    slot0 = [sum(len(g) for g in groups[:step]) for step in range(len(STEPS))]

    def reduce_copy(step, d):
        slot = slot0[step] + d
        return remote(sums.at[step], sums_in.at[slot], ar_send.at[slot], ar_recv.at[slot], moved(groups[step][d]))

    def reduce_send(step):
        for d in range(len(groups[step])):
            reduce_copy(step, d).start()

    def reduce_recv(step):
        tot = sums[step]
        for d in range(len(groups[step])):
            reduce_copy(step, d).wait_recv()
            tot = tot + sums_in[slot0[step] + d]
        return tot

    reduce_send(0)

    nt = (((1,), (1,)), ((), ()))
    dot = functools.partial(lax.dot_general, preferred_element_type=jnp.float32)
    local = []
    for b in range(BLOCKS):
        z, c = divmod(b, PLANE // BLKR)
        v = vec[SWEEPS, z, :, c * BLKR : (c + 1) * BLKR] * LIFT
        hi = v.astype(jnp.bfloat16)
        lo = (v - hi.astype(jnp.float32)).astype(jnp.bfloat16)
        halves[b, 0:K] = hi
        halves[b, K : 2 * K] = lo
        g = dot(hi, hi, nt) + dot(hi, lo, nt) + dot(lo, hi, nt)
        local.append(g * (1.0 / BLKR))
        if b == BLOCKS // 2 - 1:
            sums[1] = reduce_recv(0)
            reduce_send(1)

    same = [None] + [(ids[b] == ids[b - 1]).astype(jnp.float32) for b in range(1, BLOCKS)]
    run = [local[0]]
    for b in range(1, BLOCKS):
        run.append(local[b] + same[b] * run[b - 1])
    for b in range(BLOCKS - 2, -1, -1):
        run[b] = run[b] + same[b + 1] * (run[b + 1] - run[b])
    edge_out[0] = run[0]
    edge_out[1] = run[BLOCKS - 1]
    for z in range(PLANES):
        send(z, functools.partial(small_copy, z, 2))

    for z in range(PLANES):
        received(z, functools.partial(small_copy, z, 2))
    pad = jnp.zeros((K, 2 * K), jnp.float32)
    end = jnp.zeros((K, K), jnp.float32)
    for b in range(BLOCKS):
        from_left = jnp.where(id_in[0, 0:1, 0:K] == ids[b], 1.0, 0.0) * has_below
        from_right = jnp.where(id_in[1, 0:1, 0:K] == ids[b], 1.0, 0.0) * has_above
        g = run[b] + from_left * edge_in[0] + from_right * edge_in[1]
        aug[pl.ds(b, K, stride=BLOCKS), :] = jnp.concatenate([pad, g, end], axis=1)

    sums[2] = reduce_recv(1)
    reduce_send(2)

    lane = lax.broadcasted_iota(jnp.int32, (BLOCKS, 128), 1)
    r = [
        aug[i * BLOCKS : (i + 1) * BLOCKS, :] + jnp.where((lane == i) | (lane == K + i), 1.0, 0.0)
        for i in range(K)
    ]
    for k in range(K):
        d = jnp.broadcast_to(r[k][:, 2 * K + k : 2 * K + k + 1], (BLOCKS, 128))
        scaled = r[k] / d
        for i in range(k + 1, K):
            r[i] = r[i] - jnp.broadcast_to(r[k][:, 2 * K + i : 2 * K + i + 1], (BLOCKS, 128)) * scaled
        keep = (lane < 2 * K) | (lane >= 2 * K + k)
        rows[k * BLOCKS : (k + 1) * BLOCKS, :] = jnp.where(keep, r[k] * lax.rsqrt(d), 0.0)

    for b in range(BLOCKS):
        z, c = divmod(b, PLANE // BLKR)
        w = rows[pl.ds(b, K, stride=BLOCKS), :][:, 0 : 2 * K]
        hi = w.astype(jnp.bfloat16)
        lo = (w - hi.astype(jnp.float32)).astype(jnp.bfloat16)
        nn = (((1,), (0,)), ((), ()))
        x = halves[b]
        p = dot(hi, x, nn) + dot(lo, x, nn)
        for t in range(BLKR // 128):
            out[pl.ds((c * (BLKR // 128) + t) * PLANES + z, K, stride=PLANE // 128 * PLANES), :] = p[:, t * 128 : (t + 1) * 128]

    total[...] = reduce_recv(2)

    for i in range(3):
        for z in range(PLANES):
            sent(z, functools.partial(small_copy, z, i))
    for step in range(len(STEPS)):
        for d in range(len(groups[step])):
            reduce_copy(step, d).wait_send()

    def drain(t, carry):
        for z in range(PLANES):
            sent(z, functools.partial(plane_copy, lax.div(t, GROUPS), lax.rem(t, GROUPS), z))
        return carry

    lax.fori_loop(0, SWEEPS * GROUPS, drain, 0)


def finish(found, rows_in, total_in, out, coarse, rows, total, scaled, sem):
    large = pltpu.make_async_copy(found, out, sem.at[0])
    parts = [pltpu.make_async_copy(rows_in, rows, sem.at[2]), pltpu.make_async_copy(total_in, total, sem.at[3])]
    for c in parts + [large]:
        c.start()
    for c in parts:
        c.wait()
    inv = lax.rsqrt(total[0:1, 0:K] * (1.0 / CELLS) + EPS) * (1.0 / LIFT)
    for b in range(BLOCKS):
        scaled[b] = rows[pl.ds(b, K, stride=BLOCKS), :][:, 2 * K : 3 * K] * inv
    small = pltpu.make_async_copy(scaled, coarse, sem.at[1])
    small.start()
    large.wait()
    small.wait()


def lines_of(vectors):
    return jnp.transpose(vectors.reshape(K, PLANES, PLANE // 128, 128), (0, 2, 1, 3)).reshape(-1, 128)


def local(n, start_vectors, materials, conduct_table, aggregate_ids):
    f32 = jnp.float32
    slots = sum(len(peers(step)) for step in STEPS)
    lines = K * PLANES * PLANE // 128
    vmem, anywhere = pl.BlockSpec(memory_space=pltpu.VMEM), pl.BlockSpec(memory_space=pl.ANY)
    found, rows, total = pl.pallas_call(
        functools.partial(kernel, n),
        out_shape=(
            jax.ShapeDtypeStruct((lines, 128), f32),
            jax.ShapeDtypeStruct((K * BLOCKS, 128), f32),
            jax.ShapeDtypeStruct((1, 128), f32),
        ),
        in_specs=[anywhere] * 4,
        out_specs=(vmem, vmem, vmem),
        scratch_shapes=[
            pltpu.VMEM((lines, 128), f32),
            pltpu.VMEM((PLANES, PLANE), jnp.int32),
            pltpu.SMEM((NMAT,), f32),
            pltpu.SMEM((BLOCKS,), jnp.int32),
            pltpu.VMEM((SWEEPS + 1, PLANES, K, PLANE), f32),
            pltpu.VMEM((SWEEPS, 2, K, PLANE), f32),
            pltpu.VMEM((PLANES, 6, 8, PLANE), f32),
            pltpu.VMEM((PLANES, 8, PLANE), f32),
            pltpu.VMEM((PLANES, 1, PLANE), f32),
            pltpu.VMEM((2, 1, PLANE), f32),
            pltpu.VMEM((2, 8, 128), jnp.int32),
            pltpu.VMEM((2, 8, 128), jnp.int32),
            pltpu.VMEM((2, K, K), f32),
            pltpu.VMEM((2, K, K), f32),
            pltpu.VMEM((K * BLOCKS, 128), f32),
            pltpu.VMEM((BLOCKS, 2 * K, BLKR), jnp.bfloat16),
            pltpu.VMEM((K, 128), f32),
            pltpu.VMEM((len(STEPS), 1, 128), f32),
            pltpu.VMEM((slots, 1, 128), f32),
            pltpu.SemaphoreType.DMA((3 + GROUPS,)),
            pltpu.SemaphoreType.DMA((SWEEPS, GROUPS, PLANES)),
            pltpu.SemaphoreType.DMA((SWEEPS, GROUPS, PLANES)),
            pltpu.SemaphoreType.DMA((3, PLANES)),
            pltpu.SemaphoreType.DMA((3, PLANES)),
            pltpu.SemaphoreType.DMA((slots,)),
            pltpu.SemaphoreType.DMA((slots,)),
            pltpu.SemaphoreType.REGULAR((len(TOKENS), len(ENTRY))),
        ],
        compiler_params=pltpu.CompilerParams(
            collective_id=0, has_side_effects=True, vmem_limit_bytes=54840524
        ),
        name="adaptive_setup",
    )(lines_of(start_vectors), materials, conduct_table, aggregate_ids)
    out, coarse = pl.pallas_call(
        finish,
        out_shape=(jax.ShapeDtypeStruct((lines, 128), f32), jax.ShapeDtypeStruct((BLOCKS, K, K), f32)),
        in_specs=[anywhere] * 3,
        out_specs=(anywhere, anywhere),
        scratch_shapes=[
            pltpu.VMEM((K * BLOCKS, 128), f32),
            pltpu.VMEM((1, 128), f32),
            pltpu.VMEM((BLOCKS, K, K), f32),
            pltpu.SemaphoreType.DMA((4,)),
        ],
        compiler_params=pltpu.CompilerParams(vmem_limit_bytes=2 * 2**20),
        name="adaptive_finish",
    )(found, rows, total)
    out = jnp.transpose(out.reshape(K, PLANE // 128, PLANES, 128), (0, 2, 1, 3)).reshape(K, PLANES, PLANE)
    return out, coarse


def solution(mesh):
    n = mesh.shape["slab"]
    return jax.shard_map(
        functools.partial(local, n),
        mesh=mesh,
        in_specs=(P(None, "slab", None), P("slab", None), P(), P("slab")),
        out_specs=(P(None, "slab", None), P("slab", None, None)),
        check_vma=False,
    )
```

```python
import functools

import jax
import jax.numpy as jnp
from jax import lax
from jax.experimental import pallas as pl
from jax.experimental.pallas import tpu as pltpu
from jax.sharding import PartitionSpec as P

K = 32
BLKR = 512
NX = 256
NY = 16
PLANE = NX * NY
SWEEPS = 4
NMAT = 8
GROUP = 8
GROUPS = K // GROUP
BLOCKS = 16
PLANES = 2
CELLS = 1024 * PLANE

WEIGHT = 2.0 / 3.0
EPS = 1e-06
LIFT = 2.0**20


CORE, X, Y, Z = (1, 2), (2, 4), (128, 4), (8, 16)
STEPS = ((CORE,), (X, Y), (Z,))
ENTRY = ((X, 1), (X, 3), (Y, 1), (Y, 3), (Z, 1), (Z, 15))
TOKENS = (ENTRY, ((X, 1), (X, 2), (X, 3), (Z, 2), (Z, 14)), ((Z, 4), (Z, 12)))


def peers(step):
    found = [()]
    for axis in step:
        found = [f + ((axis, d),) for f in found for d in range(axis[1])]
    found.sort(key=lambda f: -sum(min(d, size - d) for (_, size), d in f))
    return [tuple(move for move in f if move[1]) for f in found if any(d for _, d in f)]


def kernel(
    n, sv, mat_hbm, table_hbm, ids_hbm, out, rows, total,
    raw, mat, table, ids, vec, halo, coef, cond, cond_out, cond_in, id_out, id_in,
    edge_out, edge_in, aug, halves, squares, sums, sums_in,
    load_sem, send_sem, recv_sem, small_send, small_recv, ar_send, ar_recv, token,
):
    me = lax.axis_index("slab")
    right, left = lax.rem(me + 1, n), lax.rem(me + n - 1, n)
    sides = (left, right)
    to_ok = (me > 0, me < n - 1)
    from_ok = (me < n - 1, me > 0)

    def moved(moves):
        dev = me
        for (stride, size), d in moves:
            pos = lax.rem(lax.div(me, stride), size)
            dev = dev + (lax.rem(pos + d, size) - pos) * stride
        return dev

    def signal(sem, dev):
        pl.semaphore_signal(sem, inc=1, device_id=(dev,), device_id_type=pl.DeviceIdType.MESH)

    def remote(src, dst, ssem, rsem, dev):
        return pltpu.make_async_remote_copy(
            src_ref=src, dst_ref=dst, send_sem=ssem, recv_sem=rsem,
            device_id=(dev,), device_id_type=pl.DeviceIdType.MESH,
        )

    barrier = pltpu.get_barrier_semaphore()
    for move in ENTRY:
        signal(barrier, moved((move,)))
    for z in range(PLANES):

        @pl.when(to_ok[z])
        def _():
            signal(barrier, sides[z])

    entries = len(ENTRY) + to_ok[0].astype(jnp.int32) + to_ok[1].astype(jnp.int32)

    first = [
        pltpu.make_async_copy(mat_hbm, mat, load_sem.at[0]),
        pltpu.make_async_copy(table_hbm, table, load_sem.at[1]),
        pltpu.make_async_copy(ids_hbm, ids, load_sem.at[2]),
    ]
    part = GROUP * PLANE // 128 * PLANES
    loads = [
        pltpu.make_async_copy(sv.at[pl.ds(q * part, part)], raw.at[pl.ds(q * part, part)], load_sem.at[3 + q])
        for q in range(GROUPS)
    ]
    for c in first + loads:
        c.start()
    for c in first:
        c.wait()

    for z in range(PLANES):
        for y in range(NY):
            cols = slice(y * NX, (y + 1) * NX)
            m = jnp.broadcast_to(mat[z : z + 1, cols], (8, NX))
            k = jnp.zeros((8, NX), jnp.float32)
            for j in range(NMAT):
                k = jnp.where(m == j, table[j], k)
            cond[z, :, cols] = k
            cond_out[z, :, cols] = k[0:1]
    id_out[0] = jnp.full((8, 128), ids[0], jnp.int32)
    id_out[1] = jnp.full((8, 128), ids[BLOCKS - 1], jnp.int32)

    pl.semaphore_wait(barrier, entries)

    def send(z, copy):
        @pl.when(to_ok[z])
        def _():
            copy().start()

    def sent(z, copy):
        @pl.when(to_ok[z])
        def _():
            copy().wait_send()

    def received(z, copy):
        @pl.when(from_ok[z])
        def _():
            copy().wait_recv()


    def small_copy(z, i):
        src, dst = ((cond_out, cond_in), (id_out, id_in), (edge_out, edge_in))[i]
        return remote(src.at[z], dst.at[1 - z], small_send.at[i, z], small_recv.at[i, z], sides[z])

    for i in range(2):
        for z in range(PLANES):
            send(z, functools.partial(small_copy, z, i))

    def plane_copy(s, q, z):
        lanes = pl.ds(pl.multiple_of(q * GROUP, GROUP), GROUP)
        return remote(
            vec.at[s, z, lanes], halo.at[s, 1 - z, lanes],
            send_sem.at[s, q, z], recv_sem.at[s, q, z], sides[z],
        )

    for q in range(GROUPS):
        loads[q].wait()
        for z in range(PLANES):
            for t in range(PLANE // 128):
                vec[0, z, q * GROUP : (q + 1) * GROUP, t * 128 : (t + 1) * 128] = raw[
                    pl.ds(q * part + t * PLANES + z, GROUP, stride=PLANE // 128 * PLANES), :
                ]
            send(z, functools.partial(plane_copy, 0, q, z))

    def pass_token(turn):
        for i, move in enumerate(TOKENS[turn]):
            signal(token.at[turn, i], moved((move,)))

    def take_token(turn):
        for i in range(len(TOKENS[turn])):
            pl.semaphore_wait(token.at[turn, i], 1)

    pass_token(0)

    for z in range(PLANES):

        @pl.when(jnp.logical_not(from_ok[z]))
        def _():
            cond_in[1 - z] = jnp.zeros((1, PLANE), jnp.float32)
            id_in[1 - z] = jnp.zeros((8, 128), jnp.int32)
            edge_in[1 - z] = jnp.zeros((K, K), jnp.float32)

            def clear(t, carry):
                s, q = lax.div(t, GROUPS), lax.rem(t, GROUPS)
                lanes = pl.ds(pl.multiple_of(q * GROUP, GROUP), GROUP)
                halo[s, 1 - z, lanes] = jnp.zeros((GROUP, PLANE), jnp.float32)
                return carry

            lax.fori_loop(0, SWEEPS * GROUPS, clear, 0)

    for i in range(2):
        for z in range(PLANES):
            received(z, functools.partial(small_copy, z, i))

    has_below = (me > 0).astype(jnp.float32)
    has_above = (me < n - 1).astype(jnp.float32)
    xpos = lax.broadcasted_iota(jnp.int32, (8, NX), 1)
    west_ok, east_ok = xpos > 0, xpos < NX - 1

    def face(k, other):
        return 2.0 * k * other / (k + other)

    for z in range(PLANES):
        for y in range(NY):
            cols = slice(y * NX, (y + 1) * NX)
            k = cond[z, :, cols]
            zero = jnp.zeros_like(k)
            fw = face(k, pltpu.roll(k, 1, axis=1))
            fe = face(k, pltpu.roll(k, NX - 1, axis=1))
            fs = face(k, cond[z, :, (y - 1) * NX : y * NX]) if y > 0 else k
            fn = face(k, cond[z, :, (y + 1) * NX : (y + 2) * NX]) if y < NY - 1 else k
            below = cond[0, :, cols] if z == 1 else jnp.broadcast_to(cond_in[0, :, cols], (8, NX))
            above = cond[1, :, cols] if z == 0 else jnp.broadcast_to(cond_in[1, :, cols], (8, NX))
            fd, fu = face(k, below), face(k, above)
            hd = has_below if z == 0 else 1.0
            hu = has_above if z == 1 else 1.0
            dsum = (
                jnp.where(west_ok, fw, k) + jnp.where(east_ok, fe, k) + fs + fn
                + (hd * fd + (1.0 - hd) * k) + (hu * fu + (1.0 - hu) * k)
            )
            scale = WEIGHT / dsum
            coef[z, 0, :, cols] = jnp.where(west_ok, fw * scale, zero)
            coef[z, 1, :, cols] = jnp.where(east_ok, fe * scale, zero)
            coef[z, 2, :, cols] = fs * scale
            coef[z, 3, :, cols] = fn * scale
            coef[z, 4, :, cols] = fd * scale * hd
            coef[z, 5, :, cols] = fu * scale * hu

    def sweep(t, carry):
        s, q = lax.div(t, GROUPS), lax.rem(t, GROUPS)
        lanes = pl.ds(pl.multiple_of(q * GROUP, GROUP), GROUP)
        for z in range(PLANES):
            received(z, functools.partial(plane_copy, s, q, z))
        square = jnp.zeros((GROUP, NX), jnp.float32)
        for z in range(PLANES):
            for y in range(NY):
                cols = slice(y * NX, (y + 1) * NX)
                c = vec[s, z, lanes, cols]
                acc = c * (1.0 - WEIGHT)
                acc += coef[z, 0, :, cols] * pltpu.roll(c, 1, axis=1)
                acc += coef[z, 1, :, cols] * pltpu.roll(c, NX - 1, axis=1)
                if y > 0:
                    acc += coef[z, 2, :, cols] * vec[s, z, lanes, (y - 1) * NX : y * NX]
                if y < NY - 1:
                    acc += coef[z, 3, :, cols] * vec[s, z, lanes, (y + 1) * NX : (y + 2) * NX]
                below = vec[s, 0, lanes, cols] if z == 1 else halo[s, 0, lanes, cols]
                above = vec[s, 1, lanes, cols] if z == 0 else halo[s, 1, lanes, cols]
                acc += coef[z, 4, :, cols] * below
                acc += coef[z, 5, :, cols] * above
                vec[s + 1, z, lanes, cols] = acc
                square += acc * acc

            @pl.when((s < SWEEPS - 1) & to_ok[z])
            def _():
                plane_copy(s + 1, q, z).start()

        squares[lanes, :] = square[:, 0:128] + square[:, 128:NX]
        return carry

    lax.fori_loop(0, GROUPS, sweep, 0)
    take_token(0)
    pass_token(1)
    lax.fori_loop(GROUPS, 2 * GROUPS, sweep, 0)
    take_token(1)
    pass_token(2)
    lax.fori_loop(2 * GROUPS, SWEEPS * GROUPS, sweep, 0)
    take_token(2)

    i_pos = lax.broadcasted_iota(jnp.int32, (K, 128), 0)
    j_pos = lax.broadcasted_iota(jnp.int32, (K, 128), 1)
    each = jnp.sum(squares[...], axis=1, keepdims=True)
    row = jnp.sum(jnp.where(i_pos == j_pos, each, 0.0), axis=0, keepdims=True)
    sums[0] = row

    groups = [peers(step) for step in STEPS]
    slot0 = [sum(len(g) for g in groups[:step]) for step in range(len(STEPS))]

    def reduce_copy(step, d):
        slot = slot0[step] + d
        return remote(sums.at[step], sums_in.at[slot], ar_send.at[slot], ar_recv.at[slot], moved(groups[step][d]))

    def reduce_send(step):
        for d in range(len(groups[step])):
            reduce_copy(step, d).start()

    def reduce_recv(step):
        tot = sums[step]
        for d in range(len(groups[step])):
            reduce_copy(step, d).wait_recv()
            tot = tot + sums_in[slot0[step] + d]
        return tot

    reduce_send(0)

    nt = (((1,), (1,)), ((), ()))
    dot = functools.partial(lax.dot_general, preferred_element_type=jnp.float32)
    local = []
    for b in range(BLOCKS):
        z, c = divmod(b, PLANE // BLKR)
        v = vec[SWEEPS, z, :, c * BLKR : (c + 1) * BLKR] * LIFT
        hi = v.astype(jnp.bfloat16)
        lo = (v - hi.astype(jnp.float32)).astype(jnp.bfloat16)
        halves[b, 0:K] = hi
        halves[b, K : 2 * K] = lo
        g = dot(hi, hi, nt) + dot(hi, lo, nt) + dot(lo, hi, nt)
        local.append(g * (1.0 / BLKR))
        if b == BLOCKS // 2 - 1:
            sums[1] = reduce_recv(0)
            reduce_send(1)

    same = [None] + [(ids[b] == ids[b - 1]).astype(jnp.float32) for b in range(1, BLOCKS)]
    run = [local[0]]
    for b in range(1, BLOCKS):
        run.append(local[b] + same[b] * run[b - 1])
    for b in range(BLOCKS - 2, -1, -1):
        run[b] = run[b] + same[b + 1] * (run[b + 1] - run[b])
    edge_out[0] = run[0]
    edge_out[1] = run[BLOCKS - 1]
    for z in range(PLANES):
        send(z, functools.partial(small_copy, z, 2))

    for z in range(PLANES):
        received(z, functools.partial(small_copy, z, 2))
    pad = jnp.zeros((K, 2 * K), jnp.float32)
    end = jnp.zeros((K, K), jnp.float32)
    for b in range(BLOCKS):
        from_left = jnp.where(id_in[0, 0:1, 0:K] == ids[b], 1.0, 0.0) * has_below
        from_right = jnp.where(id_in[1, 0:1, 0:K] == ids[b], 1.0, 0.0) * has_above
        g = run[b] + from_left * edge_in[0] + from_right * edge_in[1]
        aug[pl.ds(b, K, stride=BLOCKS), :] = jnp.concatenate([pad, g, end], axis=1)

    sums[2] = reduce_recv(1)
    reduce_send(2)

    lane = lax.broadcasted_iota(jnp.int32, (BLOCKS, 128), 1)
    r = [
        aug[i * BLOCKS : (i + 1) * BLOCKS, :] + jnp.where((lane == i) | (lane == K + i), 1.0, 0.0)
        for i in range(K)
    ]
    for k in range(K):
        d = jnp.broadcast_to(r[k][:, 2 * K + k : 2 * K + k + 1], (BLOCKS, 128))
        scaled = r[k] / d
        for i in range(k + 1, K):
            r[i] = r[i] - jnp.broadcast_to(r[k][:, 2 * K + i : 2 * K + i + 1], (BLOCKS, 128)) * scaled
        keep = (lane < 2 * K) | (lane >= 2 * K + k)
        rows[k * BLOCKS : (k + 1) * BLOCKS, :] = jnp.where(keep, r[k] * lax.rsqrt(d), 0.0)

    for b in range(BLOCKS):
        z, c = divmod(b, PLANE // BLKR)
        w = rows[pl.ds(b, K, stride=BLOCKS), :][:, 0 : 2 * K]
        hi = w.astype(jnp.bfloat16)
        lo = (w - hi.astype(jnp.float32)).astype(jnp.bfloat16)
        nn = (((1,), (0,)), ((), ()))
        x = halves[b]
        p = dot(hi, x, nn) + dot(lo, x, nn)
        for t in range(BLKR // 128):
            out[pl.ds((c * (BLKR // 128) + t) * PLANES + z, K, stride=PLANE // 128 * PLANES), :] = p[:, t * 128 : (t + 1) * 128]

    for i in range(3):
        for z in range(PLANES):
            sent(z, functools.partial(small_copy, z, i))
    for step in range(len(STEPS)):
        for d in range(len(groups[step])):
            reduce_copy(step, d).wait_send()

    def drain(t, carry):
        for z in range(PLANES):
            sent(z, functools.partial(plane_copy, lax.div(t, GROUPS), lax.rem(t, GROUPS), z))
        return carry

    lax.fori_loop(0, SWEEPS * GROUPS, drain, 0)

    total[...] = reduce_recv(2)


def finish(found, rows_in, total_in, out, coarse, rows, total, scaled, sem):
    large = pltpu.make_async_copy(found, out, sem.at[0])
    parts = [pltpu.make_async_copy(rows_in, rows, sem.at[2]), pltpu.make_async_copy(total_in, total, sem.at[3])]
    for c in parts + [large]:
        c.start()
    for c in parts:
        c.wait()
    inv = lax.rsqrt(total[0:1, 0:K] * (1.0 / CELLS) + EPS) * (1.0 / LIFT)
    for b in range(BLOCKS):
        scaled[b] = rows[pl.ds(b, K, stride=BLOCKS), :][:, 2 * K : 3 * K] * inv
    small = pltpu.make_async_copy(scaled, coarse, sem.at[1])
    small.start()
    large.wait()
    small.wait()


def lines_of(vectors):
    return jnp.transpose(vectors.reshape(K, PLANES, PLANE // 128, 128), (0, 2, 1, 3)).reshape(-1, 128)


def local(n, start_vectors, materials, conduct_table, aggregate_ids):
    f32 = jnp.float32
    slots = sum(len(peers(step)) for step in STEPS)
    lines = K * PLANES * PLANE // 128
    vmem, anywhere = pl.BlockSpec(memory_space=pltpu.VMEM), pl.BlockSpec(memory_space=pl.ANY)
    found, rows, total = pl.pallas_call(
        functools.partial(kernel, n),
        out_shape=(
            jax.ShapeDtypeStruct((lines, 128), f32),
            jax.ShapeDtypeStruct((K * BLOCKS, 128), f32),
            jax.ShapeDtypeStruct((1, 128), f32),
        ),
        in_specs=[anywhere] * 4,
        out_specs=(vmem, vmem, vmem),
        scratch_shapes=[
            pltpu.VMEM((lines, 128), f32),
            pltpu.VMEM((PLANES, PLANE), jnp.int32),
            pltpu.SMEM((NMAT,), f32),
            pltpu.SMEM((BLOCKS,), jnp.int32),
            pltpu.VMEM((SWEEPS + 1, PLANES, K, PLANE), f32),
            pltpu.VMEM((SWEEPS, 2, K, PLANE), f32),
            pltpu.VMEM((PLANES, 6, 8, PLANE), f32),
            pltpu.VMEM((PLANES, 8, PLANE), f32),
            pltpu.VMEM((PLANES, 1, PLANE), f32),
            pltpu.VMEM((2, 1, PLANE), f32),
            pltpu.VMEM((2, 8, 128), jnp.int32),
            pltpu.VMEM((2, 8, 128), jnp.int32),
            pltpu.VMEM((2, K, K), f32),
            pltpu.VMEM((2, K, K), f32),
            pltpu.VMEM((K * BLOCKS, 128), f32),
            pltpu.VMEM((BLOCKS, 2 * K, BLKR), jnp.bfloat16),
            pltpu.VMEM((K, 128), f32),
            pltpu.VMEM((len(STEPS), 1, 128), f32),
            pltpu.VMEM((slots, 1, 128), f32),
            pltpu.SemaphoreType.DMA((3 + GROUPS,)),
            pltpu.SemaphoreType.DMA((SWEEPS, GROUPS, PLANES)),
            pltpu.SemaphoreType.DMA((SWEEPS, GROUPS, PLANES)),
            pltpu.SemaphoreType.DMA((3, PLANES)),
            pltpu.SemaphoreType.DMA((3, PLANES)),
            pltpu.SemaphoreType.DMA((slots,)),
            pltpu.SemaphoreType.DMA((slots,)),
            pltpu.SemaphoreType.REGULAR((len(TOKENS), len(ENTRY))),
        ],
        compiler_params=pltpu.CompilerParams(
            collective_id=0, has_side_effects=True, vmem_limit_bytes=54840524
        ),
        name="adaptive_setup",
    )(lines_of(start_vectors), materials, conduct_table, aggregate_ids)
    out, coarse = pl.pallas_call(
        finish,
        out_shape=(jax.ShapeDtypeStruct((lines, 128), f32), jax.ShapeDtypeStruct((BLOCKS, K, K), f32)),
        in_specs=[anywhere] * 3,
        out_specs=(anywhere, anywhere),
        scratch_shapes=[
            pltpu.VMEM((K * BLOCKS, 128), f32),
            pltpu.VMEM((1, 128), f32),
            pltpu.VMEM((BLOCKS, K, K), f32),
            pltpu.SemaphoreType.DMA((4,)),
        ],
        compiler_params=pltpu.CompilerParams(vmem_limit_bytes=2 * 2**20),
        name="adaptive_finish",
    )(found, rows, total)
    out = jnp.transpose(out.reshape(K, PLANE // 128, PLANES, 128), (0, 2, 1, 3)).reshape(K, PLANES, PLANE)
    return out, coarse


def solution(mesh):
    n = mesh.shape["slab"]
    return jax.shard_map(
        functools.partial(local, n),
        mesh=mesh,
        in_specs=(P(None, "slab", None), P("slab", None), P(), P("slab")),
        out_specs=(P(None, "slab", None), P("slab", None, None)),
        check_vma=False,
    )
```
